256 devices in a mesh: tm: 64 (over x_lo, y, z), head: 4 (over x_hi, core).
Axes of the slice: x: 4 (x_hi: 2, x_lo: 2; x = x_hi * 2 + x_lo), y: 4, z: 8, core: 2. Of those that a mesh axis runs over, the one named last changes fastest.
Arguments:
- frames_in: bfloat16 [256, 256, 512], P('tm'), may hold values from -6 to 6
- norm_gain: float32 [512], replicated, may hold values from 0.1 to 1.9
- w_qkv: bfloat16 [512, 3, 512], P(None, None, 'head'), may hold values from -0.25 to 0.25
- qk_scale: float32 [8], P('head'), may hold values from 0.5 to 4
- w_out: bfloat16 [512, 512], P('head'), may hold values from -0.25 to 0.25
- w_act: float32 [2, 512, 4], P(None, 'head'), may hold values from -3 to 3
- action_codes: int32 [256], P('tm'), may hold values from 0 to 999
- episode_ids: int32 [256], replicated, may hold values from 0 to 3, never falling along the last dimension, each value on 1 to 128 neighbouring positions
- cotangent: bfloat16 [256, 256, 512], P('tm', None, 'head'), may hold values from -6 to 6
- action_cotangent: float32 [256, 4], P('tm'), may hold values from -192 to 192
Outputs:
- encoded: bfloat16 [256, 256, 512], P('tm', None, 'head')
- quant_gap: float32 [256, 4], P('tm')
- grad_frames: bfloat16 [256, 256, 512], P('tm', None, 'head')
- grad_gain: float32 [512], P('head')
- grad_qkv: float32 [512, 3, 512], P(None, None, 'head')
- grad_qk_scale: float32 [8], P('head')
- grad_out: float32 [512, 512], P('head')
- grad_act: float32 [2, 512, 4], P(None, 'head')
The draws below stay inside these ranges and needn't reach their ends.
Inputs may be any that keep to these rules, and one draw needn't show every extreme that they name: `action_codes`: each frame's action code; digit l in the radix 8, 5, 5, 5, lowest first, picks the level of dimension l. `episode_ids`: never falls from one frame to the next; each episode is one run of 1 to 128 frames, and one run is exactly 128 frames long.
All inputs are finite; a program needn't handle non-finite values.
Results may differ from the reference program's by a relative error of at most 0.025.
Values may be sent and summed in bfloat16 or wider, within the bound.
No kernel may reach another device: no remote copies, remote signals or barrier semaphores. Data moves between devices by JAX's collectives and lax.ppermute only.
A program may use at most 64 MiB of HBM per device.

```python
import math
import jax
import jax.numpy as jnp
import numpy as np
from jax import lax

D = 512
H = 8
HD = 64
P_SIZE = 256
F = 256
LAG = 16
EPISODES = 4
LEVELS = 4
CODES = 1000


def with_ends(values, key, smallest, high):
    extent = values.shape
    index_at = [jax.random.randint(jax.random.fold_in(key, axis), (), 0, extent[axis]) for axis in range(len(extent))]
    values = values.at[tuple(index_at)].set(smallest)
    longest = extent.index(max(extent))
    index_at[longest] = (index_at[longest] + 1) % extent[longest]
    return values.at[tuple(index_at)].set(high)


def level_of(stream_key, dims, cuts, smallest, high):
    factor_of, own = 1.0, jax.random.fold_in(stream_key, 6)
    for axis_at, blocks in cuts:
        steps = jnp.exp(jax.random.uniform(jax.random.fold_in(own, axis_at), (blocks,), jnp.float32, smallest / len(cuts), high / len(cuts)))
        factor_of = factor_of * jnp.repeat(steps, dims[axis_at] // blocks).reshape([-1 if axis == axis_at else 1 for axis in range(len(dims))])
    return factor_of


def length_profile(count, total, bound, slope):
    portions = [(1 << 20) // math.isqrt(rank ** slope) + 1 for rank in range(2, count + 1)]
    rest, holding = total - bound - (count - 1), [1] * (count - 1)
    while rest > 0:
        candidates = [i for i in range(count - 1) if holding[i] < bound]
        pool, left = sum([portions[i] for i in candidates]), rest
        for i in candidates:
            addition = min(bound - holding[i], max(1, left * portions[i] // pool), rest)
            holding[i] = holding[i] + addition
            rest = rest - addition
    return np.array([bound] + holding)


def ragged_sizes(key, amount, total, bound, slope):
    if amount == 2:
        one = jax.random.randint(key, (), max(1, total - bound), min(bound, total - 1) + 1)
        return jnp.stack([one, total - one])
    lengths = jnp.asarray(length_profile(amount, total, bound, slope), jnp.int32)
    couples = (amount - 1) // 2
    donor, taker = lengths[1:1 + 2 * couples:2], lengths[2:2 + 2 * couples:2]
    room = jnp.minimum(donor - 1, bound - taker)
    moved = jax.random.randint(jax.random.fold_in(key, 1), (couples,), 0, 1 << 20) % (room + 1)
    lengths = lengths.at[1:1 + 2 * couples:2].set(donor - moved).at[2:2 + 2 * couples:2].set(taker + moved)
    return lengths[jax.random.permutation(jax.random.fold_in(key, 2), amount)]


def bell_draw(own_key, dims, width, bound, shards=(), kind=jnp.bfloat16):
    values = jax.random.normal(own_key, dims, jnp.float32) * width
    if len(shards) > 0:
        values = level_of(own_key, dims, shards, -0.22, 0.18) * values
    return jnp.clip(values, min=-bound, max=bound).astype(kind)


def setup_inputs(seed: int = 0) -> dict:
    streams_of = jax.random.split(jax.random.key(seed), 11)
    frames_in = bell_draw(streams_of[0], (F, P_SIZE, D), 1.0, 6.0, ((0, 64),))
    norm_gain = jnp.clip(1.0 + 0.18 * jax.random.normal(streams_of[1], (D,), jnp.float32), 0.1, 1.9)
    w_qkv = bell_draw(streams_of[2], (D, 3, H * HD), D ** -0.5, 0.25, ((2, 4),))
    qk_scale = jnp.clip(jnp.exp(math.log(4.0) - 2.0794415 * jax.random.uniform(streams_of[3], (H,), jnp.float32) ** level_of(streams_of[3], (H,), ((0, 4),), -0.2, 0.2)), 0.5, 4.0)
    w_out = bell_draw(streams_of[4], (H * HD, D), (H * HD) ** -0.5, 0.25, ((0, 4),))
    w_act = bell_draw(streams_of[5], (2, D, LEVELS), 0.5, 3.0, ((1, 4),), jnp.float32)
    action_codes = with_ends(jax.random.randint(streams_of[6], (F,), 0, CODES), jax.random.fold_in(streams_of[6], 1), 0, CODES - 1).astype(jnp.int32)
    episode_ids = jnp.searchsorted(jnp.cumsum(ragged_sizes(streams_of[7], EPISODES, F, F // 2, 0)), jnp.arange(F), side="right").astype(jnp.int32)
    cotangent = bell_draw(streams_of[8], (F, P_SIZE, D), 1.0, 6.0, ((0, 64), (2, 4)))
    action_cotangent = bell_draw(streams_of[9], (F, LEVELS), 32.0, 192.0, ((0, 64),), jnp.float32)
    return dict(frames_in=frames_in, norm_gain=norm_gain, w_qkv=w_qkv, qk_scale=qk_scale, w_out=w_out, w_act=w_act, action_codes=action_codes, episode_ids=episode_ids, cotangent=cotangent, action_cotangent=action_cotangent)


EPS = 1e-06
HIGHEST = lax.Precision.HIGHEST

def level_tables():
    sizes_list = [8.0, 5.0, 5.0, 5.0]
    half_list = [(count - 1.0) * (1.0 - 0.001) / 2.0 for count in sizes_list]
    offset_list = [0.5 if int(count) % 2 == 0 else 0.0 for count in sizes_list]
    shift_list = [0.5 * math.log((half_list[i] + offset_list[i]) / (half_list[i] - offset_list[i])) for i in range(4)]
    width_list = [float(int(count) // 2) for count in sizes_list]
    return (np.array(half_list), np.array(offset_list), np.array(shift_list), np.array(width_list))

def code_values(action_codes, widths):
    bases = jnp.array([1, 8, 40, 200], dtype=jnp.int32)
    radices = jnp.array([8, 5, 5, 5], dtype=jnp.int32)
    digits = action_codes[:, None] // bases[None, :] % radices[None, :]
    return (digits.astype(jnp.float32) - widths) / widths

def rms_scale(values):
    return lax.rsqrt(lax.optimization_barrier(jnp.mean(values * values, axis=-1, keepdims=True)) + EPS)

def patch_forward(query, keys, values, visible, factor):
    query_wide = query.astype(jnp.float32)
    keys_wide = keys.astype(jnp.float32)
    dots = jnp.einsum('thd,uhd->htu', query_wide, keys_wide)
    scores = dots * factor[:, None, None]
    weights = jnp.where(visible[None], jnp.exp(scores), 0.0)
    probs = weights / lax.optimization_barrier(jnp.sum(weights, axis=-1, keepdims=True))
    rounded = lax.optimization_barrier(probs.astype(jnp.bfloat16))
    mixed = jnp.einsum('htu,uhd->thd', rounded.astype(jnp.float32), values.astype(jnp.float32))
    return (mixed.astype(jnp.bfloat16), dots, probs, rounded)

def patch_backward(query, keys, values, upstream, visible, factor):
    unused, dots, probs, rounded = patch_forward(query, keys, values, visible, factor)
    query_wide = query.astype(jnp.float32)
    keys_wide = keys.astype(jnp.float32)
    upstream_wide = upstream.astype(jnp.float32)
    grad_probs = jnp.einsum('thd,uhd->htu', upstream_wide, values.astype(jnp.float32))
    grad_values = jnp.einsum('htu,thd->uhd', rounded.astype(jnp.float32), upstream_wide).astype(jnp.bfloat16)
    grad_scores = probs * (grad_probs - lax.optimization_barrier(jnp.sum(grad_probs * probs, axis=-1, keepdims=True)))
    scale_terms = lax.optimization_barrier(jnp.sum(grad_scores * dots, axis=(1, 2)))
    grad_rounded = lax.optimization_barrier(grad_scores.astype(jnp.bfloat16)).astype(jnp.float32)
    grad_query = factor[None, :, None] * jnp.einsum('htu,uhd->thd', grad_rounded, keys_wide)
    grad_keys = factor[None, :, None] * jnp.einsum('htu,thd->uhd', grad_rounded, query_wide)
    query_back = (grad_query - query_wide * lax.optimization_barrier(jnp.mean(grad_query * query_wide, axis=-1, keepdims=True))).astype(jnp.bfloat16)
    keys_back = (grad_keys - keys_wide * lax.optimization_barrier(jnp.mean(grad_keys * keys_wide, axis=-1, keepdims=True))).astype(jnp.bfloat16)
    return (query_back, keys_back, grad_values, scale_terms)

def reference(frames_in, norm_gain, w_qkv, qk_scale, w_out, w_act, action_codes, episode_ids, cotangent, action_cotangent):
    tokens = F * P_SIZE
    floats = frames_in.astype(jnp.float32)
    inverse = rms_scale(floats)
    normed = (floats * inverse * norm_gain).astype(jnp.bfloat16)
    normed_flat = normed.reshape(tokens, D)
    projected = jnp.dot(normed_flat, w_qkv.reshape(D, 3 * H * HD), preferred_element_type=jnp.float32)
    projected = projected.reshape(F, P_SIZE, 3, H, HD)
    query_raw = projected[:, :, 0]
    keys_raw = projected[:, :, 1]
    query_inv = rms_scale(query_raw)
    keys_inv = rms_scale(keys_raw)
    query = (query_raw * query_inv).astype(jnp.bfloat16)
    keys = (keys_raw * keys_inv).astype(jnp.bfloat16)
    values = projected[:, :, 2].astype(jnp.bfloat16)
    order = jnp.arange(F, dtype=jnp.int32)
    visible = jnp.logical_and(episode_ids[:, None] == episode_ids[None, :], order[None, :] <= order[:, None])
    factor = qk_scale * (1.0 / math.sqrt(HD))
    query_moved = jnp.moveaxis(query, 1, 0)
    keys_moved = jnp.moveaxis(keys, 1, 0)
    values_moved = jnp.moveaxis(values, 1, 0)

    def forward_one(inputs):
        return patch_forward(inputs[0], inputs[1], inputs[2], visible, factor)[0]
    attended = lax.map(forward_one, (query_moved, keys_moved, values_moved))
    attended_flat = jnp.moveaxis(attended, 0, 1).reshape(tokens, H * HD)
    branch = jnp.dot(attended_flat, w_out, preferred_element_type=jnp.float32).reshape(F, P_SIZE, D)
    encoded = (floats + branch).astype(jnp.bfloat16)
    pooled = lax.optimization_barrier(jnp.mean(encoded.astype(jnp.float32), axis=1))
    partner = jnp.concatenate([pooled[LAG:], jnp.zeros((LAG, D), jnp.float32)], axis=0)
    latent = jnp.dot(pooled, w_act[0], precision=HIGHEST) + jnp.dot(partner, w_act[1], precision=HIGHEST)
    half_level, offsets, shifts, widths = level_tables()
    curve = jnp.tanh(latent + shifts)
    bounded = (curve * half_level - offsets) / widths
    quant_gap = code_values(action_codes, widths) - bounded
    grad_latent = action_cotangent * (half_level / widths) * (1.0 - curve * curve)
    grad_act = jnp.stack([jnp.dot(pooled.T, grad_latent, precision=HIGHEST), jnp.dot(partner.T, grad_latent, precision=HIGHEST)]) / math.sqrt(F)
    own_part = jnp.dot(grad_latent, w_act[0].T, precision=HIGHEST)
    partner_part = jnp.dot(grad_latent, w_act[1].T, precision=HIGHEST)
    moved_part = jnp.concatenate([jnp.zeros((LAG, D), jnp.float32), partner_part[:F - LAG]], axis=0)
    grad_pooled = (own_part + moved_part) / P_SIZE
    upstream = (cotangent.astype(jnp.float32) + grad_pooled[:, None, :]).astype(jnp.bfloat16)
    upstream_flat = upstream.reshape(tokens, D)
    grad_out = jnp.dot(attended_flat.T, upstream_flat, preferred_element_type=jnp.float32) / math.sqrt(tokens)
    grad_attended = jnp.dot(upstream_flat, w_out.T, preferred_element_type=jnp.float32).astype(jnp.bfloat16)
    grad_attended = jnp.moveaxis(grad_attended.reshape(F, P_SIZE, H, HD), 1, 0)

    def backward_one(inputs):
        return patch_backward(inputs[0], inputs[1], inputs[2], inputs[3], visible, factor)
    query_back, keys_back, grad_values, scale_terms = lax.map(backward_one, (query_moved, keys_moved, values_moved, grad_attended))
    grad_qk_scale = lax.optimization_barrier(jnp.sum(scale_terms, axis=0)) / math.sqrt(HD) / math.sqrt(tokens)
    grad_query = query_inv * jnp.moveaxis(query_back, 0, 1).astype(jnp.float32)
    grad_keys = keys_inv * jnp.moveaxis(keys_back, 0, 1).astype(jnp.float32)
    grad_vals = jnp.moveaxis(grad_values, 0, 1).astype(jnp.float32)
    grad_projected = jnp.stack([grad_query, grad_keys, grad_vals], axis=2).astype(jnp.bfloat16).reshape(tokens, 3 * H * HD)
    grad_qkv = jnp.dot(normed_flat.T, grad_projected, preferred_element_type=jnp.float32).reshape(D, 3, H * HD) / math.sqrt(tokens)
    grad_normed = jnp.dot(grad_projected, w_qkv.reshape(D, 3 * H * HD).T, preferred_element_type=jnp.float32).reshape(F, P_SIZE, D)
    scaled = norm_gain * grad_normed
    row_dot = lax.optimization_barrier(jnp.mean(scaled * floats, axis=-1, keepdims=True))
    grad_floats = inverse * scaled - floats * inverse * inverse * inverse * row_dot
    grad_gain = lax.optimization_barrier(jnp.sum(grad_normed * floats * inverse, axis=(0, 1))) / math.sqrt(tokens)
    grad_frames = (upstream.astype(jnp.float32) + grad_floats).astype(jnp.bfloat16)
    return (encoded, quant_gap, grad_frames, grad_gain, grad_qkv, grad_qk_scale, grad_out, grad_act)
```

```python
import math

import jax
import jax.numpy as jnp
import numpy as np
from jax import lax
from jax.sharding import Mesh
from jax.sharding import PartitionSpec as P

LAG = 16
EPS = 1e-06
HIGHEST = lax.Precision.HIGHEST
TM = ("xl", "y", "z")
YZ = ("y", "z")
bf16 = jnp.bfloat16
f32 = jnp.float32


def swap(value, axis):
    return lax.ppermute(value, axis, [(0, 1), (1, 0)])


def ordered(own, other, index, axis):
    first = jnp.where(index == 0, own, other)
    second = jnp.where(index == 0, other, own)
    return jnp.stack([first, second], axis=axis)


def pick(value, index, axis):
    return lax.dynamic_index_in_dim(value, index, axis, keepdims=False)


def after(value, *earlier):
    return lax.optimization_barrier((value, *earlier))[0]


def level_tables():
    sizes_list = [8.0, 5.0, 5.0, 5.0]
    half_list = [(count - 1.0) * (1.0 - 0.001) / 2.0 for count in sizes_list]
    offset_list = [0.5 if int(count) % 2 == 0 else 0.0 for count in sizes_list]
    shift_list = [
        0.5 * math.log((half_list[i] + offset_list[i]) / (half_list[i] - offset_list[i]))
        for i in range(4)
    ]
    width_list = [float(int(count) // 2) for count in sizes_list]
    return tuple(
        np.array(v, np.float32)[:, None] for v in (half_list, offset_list, shift_list, width_list)
    )


def rms_scale(values):
    return lax.rsqrt(jnp.mean(values * values, axis=-1, keepdims=True) + EPS)


def dot(a, b, ca, cb, **kw):
    return lax.dot_general(a, b, (((ca,), (cb,)), ((), ())), preferred_element_type=f32, **kw)


def local(
    frames_in,
    norm_gain,
    w_qkv,
    qk_scale,
    w_out,
    w_act,
    action_codes,
    episode_ids,
    cotangent,
    action_cotangent,
):
    fl, patches, width = frames_in.shape
    share = cotangent.shape[2]
    n_tm = lax.axis_size("xl") * lax.axis_size("y") * lax.axis_size("z")
    n_yz = lax.axis_size("y") * lax.axis_size("z")
    frames = fl * n_tm
    group = patches // 4
    tokens = frames * patches
    hd = 64
    xl, xh, core = lax.axis_index("xl"), lax.axis_index("xh"), lax.axis_index("core")
    block = xh * 2 + core
    tm = lax.axis_index(TM)

    sent = lax.dynamic_slice_in_dim(frames_in, block * group, group, 1).transpose(1, 0, 2)
    x_own = lax.all_to_all(sent, TM, 0, 0, tiled=True)
    x_own = x_own.reshape(frames, width)
    x_other = swap(x_own, "core")

    w_both = ordered(w_qkv, swap(w_qkv, "xh"), xh, 2).reshape(width, 3 * 2 * share)
    wo_both = ordered(w_out, swap(w_out, "xh"), xh, 0).reshape(2 * share, width)
    scale_both = ordered(qk_scale, swap(qk_scale, "xh"), xh, 0).reshape(4)
    act = w_act.transpose(0, 2, 1).reshape(8, share)
    act = ordered(act, swap(act, "core"), core, 0)
    act = ordered(act, swap(act, "xh"), xh, 0).reshape(4, 8, share)
    act = act.transpose(1, 0, 2).reshape(8, width)
    ac_t = action_cotangent.T
    ac_t = ordered(ac_t, swap(ac_t, "xl"), xl, 0)

    cot = cotangent.reshape(fl, 2, 2, group, share)
    got = swap(pick(cot, 1 - core, 2), "core")
    cot = ordered(pick(cot, core, 2), got, core, 3)
    got = swap(pick(cot, 1 - xh, 1), "xh")
    cot = ordered(pick(cot, xh, 1), got, xh, 2).reshape(fl, group, width)
    cot = after(cot.transpose(1, 0, 2), x_own)
    cot_own = lax.all_to_all(cot, TM, 0, 0, tiled=True).reshape(frames, width)
    cot_other = swap(cot_own, "core")

    x_two = jnp.stack([x_own, x_other])
    floats = x_two.astype(f32)
    inverse = rms_scale(floats)
    normed = (floats * inverse * norm_gain).astype(bf16)
    normed_flat = normed.reshape(2 * frames, width)
    projected = jnp.dot(normed_flat, w_both, preferred_element_type=f32)
    projected = projected.reshape(2, frames, 3, 4, hd)
    query_raw, keys_raw = projected[:, :, 0], projected[:, :, 1]
    query_inv, keys_inv = rms_scale(query_raw), rms_scale(keys_raw)
    query = (query_raw * query_inv).astype(bf16)
    keys = (keys_raw * keys_inv).astype(bf16)
    values = projected[:, :, 2].astype(bf16)
    order = jnp.arange(frames, dtype=jnp.int32)
    visible = jnp.logical_and(
        episode_ids[:, None] == episode_ids[None, :], order[None, :] <= order[:, None]
    )
    factor = scale_both * (1.0 / math.sqrt(hd))
    dots = jnp.einsum("pthd,puhd->phtu", query, keys, preferred_element_type=f32)
    scores = dots * factor[None, :, None, None]
    weights = jnp.where(visible[None, None], jnp.exp(scores), 0.0)
    probs = weights / jnp.sum(weights, axis=-1, keepdims=True)
    rounded = probs.astype(bf16)
    attended = jnp.einsum("phtu,puhd->pthd", rounded, values, preferred_element_type=f32)
    attended = attended.astype(bf16).reshape(2, frames, 2 * share)

    act_out = dot(act, wo_both.astype(f32), 1, 1, precision=HIGHEST)
    pooled_att = attended[0].astype(f32) + attended[1].astype(f32)
    terms = dot(act_out, pooled_att, 1, 1, precision=HIGHEST)
    terms = terms + dot(act, floats[0], 1, 1, precision=HIGHEST)
    terms = terms * (1.0 / patches)
    part = terms[:4] + jnp.pad(terms[4:, LAG:], ((0, 0), (0, LAG)))
    for axis in ("core", "xh", "xl"):
        part = part + swap(part, axis)
    part = part.reshape(4, 2, frames // 2)
    packed = jnp.concatenate(
        [part.reshape(8, frames // 2), jnp.pad(ac_t.reshape(8, fl), ((0, 0), (0, frames // 2 - fl)))]
    )
    packed = after(packed, cot_own)
    packed = jnp.broadcast_to(packed[None], (n_yz, 16, frames // 2))
    packed = lax.all_to_all(packed, YZ, 0, 0, tiled=True)
    latent = jnp.sum(packed[:, :8], axis=0).reshape(4, frames)
    ac_all = packed[:, 8:, :fl].reshape(n_yz, 2, 4, fl).transpose(2, 1, 0, 3).reshape(4, frames)

    half_level, offsets, shifts, widths = level_tables()
    curve = jnp.tanh(latent + shifts)
    bounded = (curve * half_level - offsets) / widths
    bases = jnp.array([1, 8, 40, 200], dtype=jnp.int32)[:, None]
    radices = jnp.array([8, 5, 5, 5], dtype=jnp.int32)[:, None]
    digits = action_codes[None, :] // bases % radices
    bounded_own = lax.dynamic_slice_in_dim(bounded, tm * fl, fl, 1)
    quant_gap = ((digits.astype(f32) - widths) / widths - bounded_own).T
    grad_latent = ac_all * (half_level / widths) * (1.0 - curve * curve)
    moved = jnp.pad(grad_latent[:, : frames - LAG], ((0, 0), (LAG, 0)))
    grad_eight = jnp.concatenate([grad_latent, moved])
    grad_pooled = dot(grad_eight, act, 0, 0, precision=HIGHEST) * (1.0 / patches)

    branch = jnp.dot(
        attended.reshape(2 * frames, 2 * share), wo_both, preferred_element_type=f32
    ).reshape(2, frames, width)
    got = swap(branch[1].astype(bf16), "core").astype(f32)
    encoded_own = (floats[0] + (branch[0] + got)).astype(bf16)

    def home(value, *earlier):
        value = after(value.reshape(n_tm, fl, width), *earlier)
        value = lax.all_to_all(value, TM, 0, 0, tiled=True)
        value = value.reshape(group, fl, 2, 2, share)
        got = swap(pick(value, 1 - xh, 2), "xh")
        value = ordered(pick(value, xh, 2), got, xh, 0)
        got = swap(pick(value, 1 - core, 3), "core")
        value = ordered(pick(value, core, 3), got, core, 1)
        return value.transpose(3, 0, 1, 2, 4).reshape(fl, patches, share)

    encoded = home(encoded_own, latent)

    upstream = (
        jnp.stack([cot_own, cot_other]).astype(f32) + grad_pooled[None]
    ).astype(bf16)
    upstream_flat = upstream.reshape(2 * frames, width)
    attended_flat = attended.reshape(2 * frames, 2 * share)
    grad_out_part = dot(attended_flat, upstream_flat, 0, 0)
    grad_att = dot(upstream_flat, wo_both, 1, 1).astype(bf16).reshape(2, frames, 4, hd)
    grad_probs = jnp.einsum("pthd,puhd->phtu", grad_att, values, preferred_element_type=f32)
    grad_values = jnp.einsum("phtu,pthd->puhd", rounded, grad_att, preferred_element_type=f32)
    grad_scores = probs * (grad_probs - jnp.sum(grad_probs * probs, axis=-1, keepdims=True))
    grad_rounded = grad_scores.astype(bf16)
    grad_query = jnp.einsum("phtu,puhd->pthd", grad_rounded, keys, preferred_element_type=f32)
    grad_keys = jnp.einsum("phtu,pthd->puhd", grad_rounded, query, preferred_element_type=f32)
    query_mean = jnp.mean(grad_query * query, axis=-1, keepdims=True)
    keys_mean = jnp.mean(grad_keys * keys, axis=-1, keepdims=True)
    scale_part = jnp.sum(query_mean, axis=(0, 1, 3)) * hd
    head_factor = factor[None, None, :, None]
    grad_query = head_factor * query_inv * (grad_query - query * query_mean)
    grad_keys = head_factor * keys_inv * (grad_keys - keys * keys_mean)
    grad_projected = jnp.stack(
        [grad_query.astype(bf16), grad_keys.astype(bf16), grad_values.astype(bf16)], axis=2
    ).reshape(2 * frames, 6 * share)
    grad_qkv_part = dot(normed_flat, grad_projected, 0, 0)
    grad_normed = dot(grad_projected, w_both, 1, 1).reshape(2, frames, width)
    got = swap(grad_normed[1].astype(bf16), "core").astype(f32)
    grad_normed = grad_normed[0] + got
    inv_own = inverse[0]
    scaled = norm_gain * grad_normed
    row_dot = jnp.mean(scaled * floats[0], axis=-1, keepdims=True)
    grad_floats = inv_own * scaled - floats[0] * (inv_own * inv_own * inv_own * row_dot)
    gain_part = jnp.sum(grad_normed * floats[0] * inv_own, axis=0)
    frames_own = (upstream[0].astype(f32) + grad_floats).astype(bf16)
    grad_frames = home(frames_own, encoded)

    qkv_blocks = grad_qkv_part.astype(bf16).reshape(2, n_yz, width // 2 // n_yz, 3, 2, share)
    out_blocks = grad_out_part.astype(bf16).reshape(2, 2, n_yz, share // 2 // n_yz, 4, share)
    act_part = dot(grad_eight, encoded_own.astype(f32), 1, 0, precision=HIGHEST)
    small = jnp.concatenate([act_part, gain_part[None]]).reshape(9, 2, 2, share)
    small = pick(small, core, 2) + swap(pick(small, 1 - core, 2), "core")
    scale_row = jnp.pad(scale_part.reshape(1, 2, 2), ((0, 0), (0, 0), (0, share - 2)))
    small = jnp.concatenate([small, scale_row])
    small_mine = pick(small, xh, 1) + swap(pick(small, 1 - xh, 1), "xh")
    small_mine = small_mine + swap(small_mine, "xl")
    qkv_mine = pick(qkv_blocks, xh, 4).astype(f32) + swap(pick(qkv_blocks, 1 - xh, 4), "xh").astype(f32)
    out_mine = pick(out_blocks, xh, 0).astype(f32) + swap(pick(out_blocks, 1 - xh, 0), "xh").astype(f32)
    rows = width // 2 // n_yz * 3
    rows_out = share // 2 // n_yz * 4
    grads = jnp.concatenate(
        [qkv_mine.reshape(2, n_yz, rows, share), out_mine.reshape(2, n_yz, rows_out, share)], axis=2
    ).astype(bf16)
    grads = pick(grads, xl, 0).astype(f32) + swap(pick(grads, 1 - xl, 0), "xl").astype(f32)

    def high_low(value):
        high = value.astype(bf16)
        return high, (value - high.astype(f32)).astype(bf16)

    high, low = high_low(small_mine)
    small_rows = jnp.pad(jnp.concatenate([high, low]), ((0, n_yz - 20), (0, 0)))
    small_rows = jnp.pad(small_rows.reshape(n_yz, 1, share), ((0, 0), (0, 7), (0, 0)))
    grads = jnp.concatenate([grads.astype(bf16), small_rows], axis=1)
    grads = after(grads, grad_frames)
    grads = lax.all_to_all(grads, YZ, 0, 0, tiled=True)
    summed = jnp.sum(grads.astype(f32), axis=0)
    high, low = high_low(summed[-8:])
    summed = jnp.concatenate([summed[:-8].astype(bf16), high[:4], low[:4]])
    summed = jnp.broadcast_to(summed[None], (n_yz, *summed.shape))
    summed = lax.all_to_all(summed, YZ, 0, 0, tiled=True)
    both = ordered(summed, swap(summed, "xl"), xl, 0).astype(f32)
    norm_factor = 1.0 / math.sqrt(tokens)
    grad_qkv = both[:, :, :rows].reshape(width, 3, share) * norm_factor
    grad_out = both[:, :, rows : rows + rows_out].reshape(share, width) * norm_factor
    last = rows + rows_out
    small_all = summed[:, last].astype(f32) + summed[:, last + 4].astype(f32)
    small_all = small_all[:10] + small_all[10:20]
    grad_act = small_all[:8].reshape(2, 4, share).transpose(0, 2, 1) * (
        1.0 / math.sqrt(frames) / patches
    )
    grad_gain = small_all[8] * norm_factor
    grad_qk_scale = small_all[9, :2] * (norm_factor / math.sqrt(hd))
    return (encoded, quant_gap, grad_frames, grad_gain, grad_qkv, grad_qk_scale, grad_out, grad_act)


def solution(mesh):
    fine = Mesh(mesh.devices.reshape(2, 4, 8, 2, 2), ("xl", "y", "z", "xh", "core"))
    head = ("xh", "core")
    in_specs = (
        P(TM, None, None),
        P(),
        P(None, None, head),
        P(head),
        P(head, None),
        P(None, head, None),
        P(TM),
        P(),
        P(TM, None, head),
        P(TM, None),
    )
    out_specs = (
        P(TM, None, head),
        P(TM, None),
        P(TM, None, head),
        P(head),
        P(None, None, head),
        P(head),
        P(head, None),
        P(None, head, None),
    )
    return jax.shard_map(local, mesh=fine, in_specs=in_specs, out_specs=out_specs, check_vma=False)
```

```python
import math

import jax
import jax.numpy as jnp
import numpy as np
from jax import lax
from jax.experimental import pallas as pl
from jax.experimental.pallas import tpu as pltpu
from jax.sharding import Mesh
from jax.sharding import PartitionSpec as P

LAG = 16
EPS = 1e-06
HIGHEST = lax.Precision.HIGHEST
TM = ("xl", "y", "z")
YZ = ("y", "z")
bf16 = jnp.bfloat16
f32 = jnp.float32
FORWARD_FLOPS = 1_000
BACKWARD_FLOPS = 5_000_000_000


def swap(value, axis):
    return lax.ppermute(value, axis, [(0, 1), (1, 0)])


def ordered(own, other, index, axis):
    first = jnp.where(index == 0, own, other)
    second = jnp.where(index == 0, other, own)
    return jnp.stack([first, second], axis=axis)


def pick(value, index, axis):
    return lax.dynamic_index_in_dim(value, index, axis, keepdims=False)


def after(value, *earlier):
    return lax.optimization_barrier((value, *earlier))[0]


HALF = [(n - 1.0) * (1.0 - 0.001) / 2.0 for n in (8.0, 5.0, 5.0, 5.0)]
OFFSET = [0.5, 0.0, 0.0, 0.0]
WIDTH = [4.0, 2.0, 2.0, 2.0]
SHIFT = [0.5 * math.log((a + b) / (a - b)) for a, b in zip(HALF, OFFSET)]


def by_level(values, shape):
    row = lax.broadcasted_iota(jnp.int32, shape, 0)
    return jnp.where(row == 0, values[0], values[1]).astype(f32)


def dot(a, b, ca, cb, **kw):
    return lax.dot_general(a, b, (((ca,), (cb,)), ((), ())), preferred_element_type=f32, **kw)


def per_head(values, first):
    one = jnp.sum(jnp.where(first, values, 0.0), axis=-1, keepdims=True)
    two = jnp.sum(jnp.where(first, 0.0, values), axis=-1, keepdims=True)
    return one, two


def attention_forward(b, scale, normed, w, ids_row, ids_col, qkv, invs, probs, attended):
    frames, share = qkv.shape[2:]
    hd = share // 2
    first = first_lanes(frames, share)
    t = lax.broadcasted_iota(jnp.int32, (frames, frames), 0)
    u = lax.broadcasted_iota(jnp.int32, (frames, frames), 1)
    visible = jnp.logical_and(ids_col[...] == ids_row[...], u <= t)
    for p in range(2):
        raw = dot(normed[p], w[...], 1, 0)
        parts = []
        for k in range(2):
            one = raw[:, k * share : (k + 1) * share]
            sums = per_head(one * one, first)
            inv0 = lax.rsqrt(sums[0] * (1.0 / hd) + EPS)
            inv1 = lax.rsqrt(sums[1] * (1.0 / hd) + EPS)
            invs[p, :, k * 2 : k * 2 + 1] = inv0
            invs[p, :, k * 2 + 1 : k * 2 + 2] = inv1
            parts.append((one * jnp.where(first, inv0, inv1)).astype(bf16))
        parts.append(raw[:, 2 * share :].astype(bf16))
        query, keys, values = parts
        for k in range(3):
            qkv[p, k] = parts[k]
        mixed = None
        zero = jnp.zeros_like(keys)
        for h in range(2):
            mask = first if h == 0 else jnp.logical_not(first)
            dots = dot(query, jnp.where(mask, keys, zero), 1, 1)
            weights = jnp.where(visible, jnp.exp(dots * (scale[b * 2 + h] * (1.0 / math.sqrt(hd)))), 0.0)
            prob = weights / jnp.sum(weights, axis=-1, keepdims=True)
            probs[p, h] = prob
            one = dot(prob.astype(bf16), jnp.where(mask, values, zero), 1, 0)
            mixed = one if mixed is None else mixed + one
        attended[p] = mixed.astype(bf16)


def forward_kernel(
    scale, x_own, x_other, gain, w_own, w_other, wo_own, wo_other, act, ids_row, ids_col,
    normed, qkv0, qkv1, invs0, invs1, probs0, probs1, attended0, attended1, enc_part, branch_other, part8,
):
    frames = x_own.shape[0]
    for p in range(2):
        x = (x_own, x_other)[p][...].astype(f32)
        inverse = lax.rsqrt(jnp.mean(x * x, axis=-1, keepdims=True) + EPS)
        normed[p] = (x * inverse * gain[...]).astype(bf16)
    attention_forward(0, scale, normed, w_own, ids_row, ids_col, qkv0, invs0, probs0, attended0)
    attention_forward(1, scale, normed, w_other, ids_row, ids_col, qkv1, invs1, probs1, attended1)
    x = x_own[...].astype(f32)
    for p in range(2):
        branch = dot(attended0[p], wo_own[...], 1, 0) + dot(attended1[p], wo_other[...], 1, 0)
        if p == 0:
            enc_part[...] = x + branch
        else:
            branch_other[...] = branch.astype(bf16)
    terms = dot(act[...], x, 1, 1, precision=HIGHEST)
    for wo, att in ((wo_own, attended0), (wo_other, attended1)):
        act_out = dot(act[...], wo[...].astype(f32), 1, 1, precision=HIGHEST)
        terms = terms + dot(act_out, att[0].astype(f32) + att[1].astype(f32), 1, 1, precision=HIGHEST)
    terms = terms * (1.0 / 256.0)
    moved = pltpu.roll(terms, frames - LAG, 1)
    moved = jnp.where(lax.broadcasted_iota(jnp.int32, moved.shape, 1) < frames - LAG, moved, 0.0)
    part = terms[:4] + moved[4:]
    part8[0:4] = part[:, : frames // 2]
    part8[4:8] = part[:, frames // 2 :]


def attention_back(b, scale, up, wo, qkv, invs, probs, gp, first):
    share = wo.shape[0]
    hd = share // 2
    sums = [None, None]
    factor = jnp.where(
        first[:1], scale[b * 2] * (1.0 / math.sqrt(hd)), scale[b * 2 + 1] * (1.0 / math.sqrt(hd))
    )
    for p in range(2):
        query, keys, values = qkv[p, 0], qkv[p, 1], qkv[p, 2]
        zero = jnp.zeros_like(keys)
        grad_att = dot(up[p], wo[...], 1, 1).astype(bf16)
        grad_q = grad_k = grad_v = None
        for h in range(2):
            mask = first if h == 0 else jnp.logical_not(first)
            grad_probs = dot(grad_att, jnp.where(mask, values, zero), 1, 1)
            prob = probs[p, h]
            inner = jnp.sum(grad_probs * prob, axis=-1, keepdims=True)
            grad_scores = (prob * (grad_probs - inner)).astype(bf16)
            one = dot(grad_scores, jnp.where(mask, keys, zero), 1, 0)
            grad_q = one if grad_q is None else grad_q + one
            one = dot(grad_scores, jnp.where(mask, query, zero), 0, 0)
            grad_k = one if grad_k is None else grad_k + one
            one = dot(prob.astype(bf16), jnp.where(mask, grad_att, zero), 0, 0)
            grad_v = one if grad_v is None else grad_v + one
        for k in range(2):
            grad, base = ((grad_q, query), (grad_k, keys))[k]
            base = base.astype(f32)
            one, two = per_head(grad * base, first)
            if k == 0:
                one_sum, two_sum = jnp.sum(one, axis=0, keepdims=True), jnp.sum(two, axis=0, keepdims=True)
                sums[0] = one_sum if sums[0] is None else sums[0] + one_sum
                sums[1] = two_sum if sums[1] is None else sums[1] + two_sum
            mean = jnp.where(first, one, two) * (1.0 / hd)
            inv = jnp.where(first, invs[p, :, 2 * k : 2 * k + 1], invs[p, :, 2 * k + 1 : 2 * k + 2])
            gp[p, :, k * share : (k + 1) * share] = (factor * inv * (grad - base * mean)).astype(bf16)
        gp[p, :, 2 * share : 3 * share] = grad_v.astype(bf16)
    lane = lax.broadcasted_iota(jnp.int32, (1, share), 1)
    return jnp.where(lane == 0, sums[0], 0.0) + jnp.where(lane == 1, sums[1], 0.0)


def weight_grads(target, normed, gp, up, attended):
    split = gp.shape[2]
    qkv_part = dot(normed[0], gp[0], 0, 0) + dot(normed[1], gp[1], 0, 0)
    out_part = dot(up[0], attended[0], 0, 0) + dot(up[1], attended[1], 0, 0)
    target[:, :split] = qkv_part.astype(target.dtype)
    target[:, split:] = out_part.astype(target.dtype)


def first_lanes(frames, share):
    return lax.broadcasted_iota(jnp.int32, (frames, share), 1) < share // 2


def other_kernel(
    scale, place, packed, cot_own, cot_other, act, wo, qkv, invs, probs, attended, normed,
    bounded_out, eight_out, up, gp, grads, scale_row,
    pooled,
):
    frames, width = up.shape[1:]
    share = wo.shape[0]
    summed = jnp.sum(packed[...], axis=0)
    latent = jnp.concatenate([summed[0:4], summed[4:8]], axis=1)
    cot_act = jnp.concatenate([summed[8:12], summed[12:16]], axis=1)
    shape = latent.shape
    half, offset, widths = by_level(HALF, shape), by_level(OFFSET, shape), by_level(WIDTH, shape)
    curve = jnp.tanh(latent + by_level(SHIFT, shape))
    bounded_out[...] = (curve * half - offset) / widths
    grad_latent = cot_act * (half / widths) * (1.0 - curve * curve)
    moved = pltpu.roll(grad_latent, LAG, 1)
    moved = jnp.where(lax.broadcasted_iota(jnp.int32, shape, 1) >= LAG, moved, 0.0)
    eight = jnp.concatenate([grad_latent, moved], axis=0)
    eight_out[...] = eight
    pooled[...] = dot(eight.T, act[...], 1, 0, precision=HIGHEST) * (1.0 / 256.0)
    xh, core = place[0], place[1]
    for p in range(2):
        core_p = core if p == 0 else 1 - core
        for r in range(4):
            block_r = (xh if r < 2 else 1 - xh) * 2 + (core_p if r % 2 == 0 else 1 - core_p)
            cols = pl.ds(pl.multiple_of(block_r * share, share), share)
            cot = (cot_own, cot_other)[p][:, r * share : (r + 1) * share].astype(f32)
            up[p, :, cols] = (cot + pooled[:, cols]).astype(bf16)
    scale_row[...] = attention_back(1, scale, up, wo, qkv, invs, probs, gp, first_lanes(frames, share))
    weight_grads(grads, normed, gp, up, attended)


def own_kernel(
    scale, place, eight, up, wo, w_own, w_other, qkv, invs, probs, attended, normed, x_own, x_other,
    encoded, gp_other, scale_other,
    grads, small, normed_own, normed_other,
    gp,
):
    frames, width = x_own.shape
    share = wo.shape[0]
    scale_own = attention_back(0, scale, up, wo, qkv, invs, probs, gp, first_lanes(frames, share))
    gain_part = None
    for p in (1, 0):
        grad = dot(gp[p], w_own[...], 1, 1) + dot(gp_other[p], w_other[...], 1, 1)
        x = (x_own, x_other)[p][...].astype(f32)
        inverse = lax.rsqrt(jnp.mean(x * x, axis=-1, keepdims=True) + EPS)
        one = jnp.sum(grad * (x * inverse), axis=0, keepdims=True)
        gain_part = one if gain_part is None else gain_part + one
        if p == 0:
            normed_own[...] = grad
        else:
            normed_other[:frames] = grad.astype(bf16)
    weight_grads(grads, normed, gp, up, attended)
    act_part = dot(eight[...], encoded[...].astype(f32), 1, 0, precision=HIGHEST)
    xh, core = place[0], place[1]
    none = jnp.zeros((1, share), f32)
    for r in range(4):
        second = (xh if r < 2 else 1 - xh) == 1
        odd = (core if r % 2 == 0 else 1 - core) == 1

        def block(value):
            low = jnp.where(odd, value[:, share : 2 * share], value[:, :share])
            high = jnp.where(odd, value[:, 3 * share :], value[:, 2 * share : 3 * share])
            return jnp.where(second, high, low)

        tail = (scale_own, none, scale_other[...], none)[r]
        rows = jnp.concatenate([block(act_part), block(gain_part), tail, jnp.zeros((6, share), f32)])
        if r == 1:
            normed_other[frames:, :share] = rows.astype(bf16)
        else:
            small[r] = rows
    small[1] = jnp.zeros((16, share), f32)
    normed_other[frames:, share:] = jnp.zeros((16, width - share), bf16)


def finish_kernel(x_own, gain, grad_own, grad_got, up, encoded, out):
    x = x_own[...].astype(f32)
    frames, width = x.shape
    inverse = lax.rsqrt(jnp.mean(x * x, axis=-1, keepdims=True) + EPS)
    scaled = gain[...] * (grad_own[...] + grad_got[:frames].astype(f32))
    row_dot = jnp.mean(scaled * x, axis=-1, keepdims=True)
    grad = inverse * scaled - x * (inverse * inverse * inverse * row_dot)
    out[:, :width] = encoded[...]
    out[:, width : 2 * width] = (up[0].astype(f32) + grad).astype(bf16)


VMEM = pl.BlockSpec(memory_space=pltpu.VMEM)
SMEM = pl.BlockSpec(memory_space=pltpu.SMEM)


def call(kernel, scalars, arrays, outs, flops, scratch=()):
    return pl.pallas_call(
        kernel,
        out_shape=[jax.ShapeDtypeStruct(s, d) for s, d in outs],
        in_specs=[SMEM] * len(scalars) + [VMEM] * len(arrays),
        out_specs=[VMEM] * len(outs),
        scratch_shapes=scratch,
        compiler_params=pltpu.CompilerParams(vmem_limit_bytes=60 * 1024 * 1024),
        cost_estimate=pl.CostEstimate(flops=flops, bytes_accessed=flops // 1000, transcendentals=0),
    )(*scalars, *arrays)


def local(
    frames_in,
    norm_gain,
    w_qkv,
    qk_scale,
    w_out,
    w_act,
    action_codes,
    episode_ids,
    cotangent,
    action_cotangent,
):
    fl, patches, width = frames_in.shape
    share = cotangent.shape[2]
    n_tm = lax.axis_size("xl") * lax.axis_size("y") * lax.axis_size("z")
    n_yz = lax.axis_size("y") * lax.axis_size("z")
    frames = fl * n_tm
    group = patches // 4
    tokens = frames * patches
    hd = 64
    xl, xh, core = lax.axis_index("xl"), lax.axis_index("xh"), lax.axis_index("core")
    block = xh * 2 + core
    tm = lax.axis_index(TM)
    gain = norm_gain.reshape(1, width)

    few = jnp.concatenate(
        [w_act.transpose(0, 2, 1).reshape(8, share), jnp.pad(qk_scale[None], ((0, 7), (0, share - 2)))]
    )
    few_got = swap(few, "core")
    few = ordered(few, few_got, core, 0)

    sent = lax.dynamic_slice_in_dim(frames_in, block * group, group, 1).transpose(1, 0, 2)
    sent = after(sent, few_got)
    x_own = lax.all_to_all(sent, TM, 0, 0, tiled=True)
    x_own = x_own.reshape(frames, width)
    x_other = swap(x_own, "core")

    w_own = w_qkv.reshape(width, 3 * share)
    w_other = swap(w_own, "xh")
    wo_other = swap(after(w_out, few_got), "xh")
    place = jnp.stack([xh, core]).astype(jnp.int32)
    few_other = swap(few, "xh")
    act = ordered(few, few_other, xh, 0).reshape(4, 16, share)[:, :8]
    act = act.transpose(1, 0, 2).reshape(8, width)
    scale = jnp.concatenate([qk_scale, pick(few_other, core, 0)[8, :2]])

    cot = after(cotangent, few_got).reshape(fl, 2, 2, group, share)
    cot = jnp.concatenate([pick(cot, core, 2), swap(pick(cot, 1 - core, 2), "core")], axis=-1)
    cot = jnp.concatenate([pick(cot, xh, 1), swap(pick(cot, 1 - xh, 1), "xh")], axis=-1)
    cot = after(cot.transpose(1, 0, 2), x_own)
    cot_own = lax.all_to_all(cot, TM, 0, 0, tiled=True).reshape(frames, width)
    cot_other = swap(cot_own, "core")

    ids_row, ids_col = episode_ids[None], episode_ids[:, None]
    (
        normed, qkv0, qkv1, invs0, invs1, probs0, probs1, attended0, attended1, enc_part, branch_other, part8
    ) = call(
        forward_kernel,
        (scale,),
        (x_own, x_other, gain, w_own, w_other, w_out, wo_other, act, ids_row, ids_col),
        (
            ((2, frames, width), bf16),
            ((2, 3, frames, share), bf16),
            ((2, 3, frames, share), bf16),
            ((2, frames, 4), f32),
            ((2, frames, 4), f32),
            ((2, 2, frames, frames), f32),
            ((2, 2, frames, frames), f32),
            ((2, frames, share), bf16),
            ((2, frames, share), bf16),
            ((frames, width), f32),
            ((frames, width), bf16),
            ((8, frames // 2), f32),
        ),
        FORWARD_FLOPS,
    )

    ac_t = jnp.broadcast_to(action_cotangent.T[:, None], (4, n_tm, fl)).reshape(4, frames)
    ac_t = jnp.where(jnp.arange(frames)[None] // fl == tm, ac_t, 0.0)
    ac8 = jnp.concatenate([ac_t[:, : frames // 2], ac_t[:, frames // 2 :]])
    part8 = part8 + swap(part8, "core")
    packed = jnp.concatenate([part8, ac8])
    from_xh = swap(part8, "xh")
    from_xl = swap(packed, "xl")
    from_both = lax.ppermute(part8, ("xl", "xh"), [(0, 3), (1, 2), (2, 1), (3, 0)])
    far = jnp.concatenate([from_xh + from_both, jnp.zeros_like(ac8)])
    packed = (packed + from_xl) + far
    packed = jnp.broadcast_to(packed[None], (n_yz, 16, frames // 2))
    packed = after(packed, cot_own)
    packed = lax.all_to_all(packed, YZ, 0, 0, tiled=True)

    encoded_own = (enc_part + swap(branch_other, "core").astype(f32)).astype(bf16)

    bounded, eight, up, gp_other, grads_other, scale_other = call(
        other_kernel,
        (scale, place),
        (packed, cot_own, cot_other, act, wo_other, qkv1, invs1, probs1, attended1, normed),
        (
            ((4, frames), f32),
            ((8, frames), f32),
            ((2, frames, width), bf16),
            ((2, frames, 3 * share), bf16),
            ((width, 4 * share), bf16),
            ((1, share), f32),
        ),
        BACKWARD_FLOPS,
        scratch=[pltpu.VMEM((frames, width), f32)],
    )
    grads_got = swap(grads_other, "xh")
    grads_own, small, normed_own, normed_other = call(
        own_kernel,
        (scale, place),
        (
            eight, up, w_out, w_own, w_other, qkv0, invs0, probs0, attended0, normed, x_own, x_other,
            encoded_own, gp_other, scale_other,
        ),
        (
            ((width, 4 * share), f32),
            ((4, 16, share), f32),
            ((frames, width), f32),
            ((frames + 16, width), bf16),
        ),
        BACKWARD_FLOPS,
        scratch=[pltpu.VMEM((2, frames, 3 * share), bf16)],
    )

    normed_got = swap(normed_other, "core")
    (both_out,) = call(
        finish_kernel,
        (),
        (x_own, gain, normed_own, normed_got, up, encoded_own),
        (((frames, 2 * width), bf16),),
        10 * frames * width,
    )
    far = lax.ppermute(small[3], ("xh", "core"), [(0, 3), (1, 2), (2, 1), (3, 0)])
    small = (small[0] + normed_got[frames:, :share].astype(f32)) + (swap(small[2], "xh") + far)
    small = jnp.pad(small.astype(bf16), ((0, frames - 16), (0, 0)))
    grads = (grads_own + grads_got.astype(f32)).astype(bf16)
    both_out = jnp.concatenate([both_out, grads[:frames], grads[frames:], small], axis=1)
    home = lax.all_to_all(both_out.reshape(n_tm, fl, 4 * width + share), TM, 0, 0, tiled=True)
    summed = jnp.sum(home[:, :, 2 * width :].astype(f32), axis=0).astype(bf16)
    summed = jnp.broadcast_to(summed[None], (n_tm, *summed.shape))
    summed = lax.all_to_all(summed, TM, 0, 0, tiled=True).reshape(frames, 2 * width + share)
    home = home[:, :, : 2 * width]
    home = home.reshape(group, fl, 2, 2, 2, share)
    got = swap(pick(home, 1 - xh, 3), "xh")
    home = ordered(pick(home, xh, 3), got, xh, 0)
    got = swap(pick(home, 1 - core, 4), "core")
    home = ordered(pick(home, core, 4), got, core, 1)
    home = home.transpose(4, 3, 0, 1, 2, 5).reshape(2, fl, patches, share)
    encoded, grad_frames = home[0], home[1]

    half_level, offsets, widths = (np.array(v, np.float32)[:, None] for v in (HALF, OFFSET, WIDTH))
    bases = jnp.array([1, 8, 40, 200], dtype=jnp.int32)[:, None]
    radices = jnp.array([8, 5, 5, 5], dtype=jnp.int32)[:, None]
    digits = action_codes[None, :] // bases % radices
    bounded_own = lax.dynamic_slice_in_dim(bounded, tm * fl, fl, 1)
    quant_gap = ((digits.astype(f32) - widths) / widths - bounded_own).T

    both = jnp.concatenate([summed[:, :width], summed[:, width : 2 * width]]).astype(f32)
    norm_factor = 1.0 / math.sqrt(tokens)
    grad_qkv = both[:, : 3 * share].reshape(width, 3, share) * norm_factor
    grad_out = both[:, 3 * share : 4 * share].T * norm_factor
    small = summed[:16, 2 * width :].astype(f32)
    grad_act = small[:8].reshape(2, 4, share).transpose(0, 2, 1) * (1.0 / math.sqrt(frames) / patches)
    grad_gain = small[8] * norm_factor
    grad_qk_scale = small[9, :2] * (norm_factor / math.sqrt(hd))
    return (encoded, quant_gap, grad_frames, grad_gain, grad_qkv, grad_qk_scale, grad_out, grad_act)


def solution(mesh):
    fine = Mesh(mesh.devices.reshape(2, 4, 8, 2, 2), ("xl", "y", "z", "xh", "core"))
    head = ("xh", "core")
    in_specs = (
        P(TM, None, None),
        P(),
        P(None, None, head),
        P(head),
        P(head, None),
        P(None, head, None),
        P(TM),
        P(),
        P(TM, None, head),
        P(TM, None),
    )
    out_specs = (
        P(TM, None, head),
        P(TM, None),
        P(TM, None, head),
        P(head),
        P(None, None, head),
        P(head),
        P(head, None),
        P(None, head, None),
    )
    return jax.shard_map(local, mesh=fine, in_specs=in_specs, out_specs=out_specs, check_vma=False)
```

```python
import math

import jax
import jax.numpy as jnp
import numpy as np
from jax import lax
from jax.experimental import pallas as pl
from jax.experimental.pallas import tpu as pltpu
from jax.sharding import Mesh
from jax.sharding import PartitionSpec as P

LAG = 16
EPS = 1e-06
HIGHEST = lax.Precision.HIGHEST
TM = ("xl", "y", "z")
YZ = ("y", "z")
bf16 = jnp.bfloat16
f32 = jnp.float32
FORWARD_FLOPS = 1_000
BACKWARD_FLOPS = 5_000_000_000


def swap(value, axis):
    return lax.ppermute(value, axis, [(0, 1), (1, 0)])


def ordered(own, other, index, axis):
    first = jnp.where(index == 0, own, other)
    second = jnp.where(index == 0, other, own)
    return jnp.stack([first, second], axis=axis)


def pick(value, index, axis):
    return lax.dynamic_index_in_dim(value, index, axis, keepdims=False)


def after(value, *earlier):
    return lax.optimization_barrier((value, *earlier))[0]


HALF = [(n - 1.0) * (1.0 - 0.001) / 2.0 for n in (8.0, 5.0, 5.0, 5.0)]
OFFSET = [0.5, 0.0, 0.0, 0.0]
WIDTH = [4.0, 2.0, 2.0, 2.0]
SHIFT = [0.5 * math.log((a + b) / (a - b)) for a, b in zip(HALF, OFFSET)]


def by_level(values, shape):
    row = lax.broadcasted_iota(jnp.int32, shape, 0)
    return jnp.where(row == 0, values[0], values[1]).astype(f32)


def dot(a, b, ca, cb, **kw):
    return lax.dot_general(a, b, (((ca,), (cb,)), ((), ())), preferred_element_type=f32, **kw)


def pieces(values):
    high = values.astype(bf16).astype(f32)
    middle = (values - high).astype(bf16).astype(f32)
    return high, middle, (values - high - middle).astype(bf16).astype(f32)


def dot_wide(few, many, ca, cb):
    rows = few.shape[0]
    out = dot(jnp.concatenate(pieces(few)).astype(bf16), many, ca, cb)
    return out[:rows] + (out[rows : 2 * rows] + out[2 * rows :])


def per_head(values, first):
    one = jnp.sum(jnp.where(first, values, 0.0), axis=-1, keepdims=True)
    two = jnp.sum(jnp.where(first, 0.0, values), axis=-1, keepdims=True)
    return one, two


def attention_forward(b, scale, normed, w, ids_row, ids_col, qkv, invs, probs, attended):
    frames, share = qkv.shape[2:]
    hd, mid = share // 2, frames // 2
    first = first_lanes(frames, share)
    t = lax.broadcasted_iota(jnp.int32, (frames, frames), 0)
    u = lax.broadcasted_iota(jnp.int32, (frames, frames), 1)
    visible = jnp.logical_and(ids_col[...] == ids_row[...], u <= t)
    for p in range(2):
        raw = dot(normed[p], w[...], 1, 0)
        parts = []
        for k in range(2):
            one = raw[:, k * share : (k + 1) * share]
            sums = per_head(one * one, first)
            inv0 = lax.rsqrt(sums[0] * (1.0 / hd) + EPS)
            inv1 = lax.rsqrt(sums[1] * (1.0 / hd) + EPS)
            invs[p, :, k * 2 : k * 2 + 1] = inv0
            invs[p, :, k * 2 + 1 : k * 2 + 2] = inv1
            parts.append((one * jnp.where(first, inv0, inv1)).astype(bf16))
        parts.append(raw[:, 2 * share :].astype(bf16))
        query, keys, values = parts
        for k in range(3):
            qkv[p, k] = parts[k]
        zero = jnp.zeros_like(keys)
        mixed = [None, None]
        for h in range(2):
            mask = first if h == 0 else jnp.logical_not(first)
            keys_h, values_h = jnp.where(mask, keys, zero), jnp.where(mask, values, zero)
            factor = scale[b * 2 + h] * (1.0 / math.sqrt(hd))
            for k, (rows, seen) in enumerate(((slice(0, mid), mid), (slice(mid, frames), frames))):
                dots = dot(query[rows], keys_h[:seen], 1, 1)
                weights = jnp.where(visible[rows, :seen], jnp.exp(dots * factor), 0.0)
                prob = weights * (1.0 / jnp.sum(weights, axis=-1, keepdims=True))
                probs[p, h, rows, :seen] = prob
                one = dot(prob.astype(bf16), values_h[:seen], 1, 0)
                mixed[k] = one if mixed[k] is None else mixed[k] + one
        attended[p] = jnp.concatenate(mixed).astype(bf16)


def forward_kernel(
    scale, in_own, in_other, gain, w_own, w_other, ids_row, ids_col, act, act_own, act_other,
    normed, qkv0, qkv1, invs0, invs1, probs0, probs1, attended0, attended1, part8,
):
    frames = in_own.shape[1]
    for p in range(2):
        x = frames_of((in_own, in_other)[p]).astype(f32)
        inverse = lax.rsqrt(jnp.mean(x * x, axis=-1, keepdims=True) + EPS)
        normed[p] = (x * inverse * gain[...]).astype(bf16)
    attention_forward(0, scale, normed, w_own, ids_row, ids_col, qkv0, invs0, probs0, attended0)
    attention_forward(1, scale, normed, w_other, ids_row, ids_col, qkv1, invs1, probs1, attended1)
    terms = dot_wide(act[...], frames_of(in_own), 1, 1)
    for act_out, att in ((act_own, attended0), (act_other, attended1)):
        terms = terms + (dot_wide(act_out[...], att[0], 1, 1) + dot_wide(act_out[...], att[1], 1, 1))
    terms = terms * (1.0 / 256.0)
    moved = pltpu.roll(terms, frames - LAG, 1)
    moved = jnp.where(lax.broadcasted_iota(jnp.int32, moved.shape, 1) < frames - LAG, moved, 0.0)
    part = terms[:4] + moved[4:]
    part8[0:4] = part[:, : frames // 2]
    part8[4:8] = part[:, frames // 2 :]


def attention_back(b, scale, up, wo, qkv, invs, probs, gp, first):
    share, frames = wo.shape[0], up.shape[1]
    hd, mid = share // 2, frames // 2
    sums = [None, None]
    factor = jnp.where(
        first[:1], scale[b * 2] * (1.0 / math.sqrt(hd)), scale[b * 2 + 1] * (1.0 / math.sqrt(hd))
    )
    for p in range(2):
        query, keys, values = qkv[p, 0], qkv[p, 1], qkv[p, 2]
        zero = jnp.zeros_like(keys)
        grad_att = dot(up[p], wo[...], 1, 1).astype(bf16)
        grad_q, low, high = [None, None], [None, None], [None, None]

        def add(old, new):
            return new if old is None else old + new

        for h in range(2):
            mask = first if h == 0 else jnp.logical_not(first)
            query_h, keys_h = jnp.where(mask, query, zero), jnp.where(mask, keys, zero)
            values_h, grad_h = jnp.where(mask, values, zero), jnp.where(mask, grad_att, zero)
            for k, (rows, seen) in enumerate(((slice(0, mid), mid), (slice(mid, frames), frames))):
                grad_probs = dot(grad_att[rows], values_h[:seen], 1, 1)
                prob = probs[p, h, rows, :seen]
                inner = jnp.sum(grad_probs * prob, axis=-1, keepdims=True)
                grad_scores = (prob * (grad_probs - inner)).astype(bf16)
                grad_q[k] = add(grad_q[k], dot(grad_scores, keys_h[:seen], 1, 0))
                target = (low, high)[k]
                target[0] = add(target[0], dot(grad_scores, query_h[rows], 0, 0))
                target[1] = add(target[1], dot(prob.astype(bf16), grad_h[rows], 0, 0))
        grad_q = jnp.concatenate(grad_q)
        grad_k, grad_v = (jnp.concatenate([low[j] + high[j][:mid], high[j][mid:]]) for j in range(2))
        for k in range(2):
            grad, base = ((grad_q, query), (grad_k, keys))[k]
            base = base.astype(f32)
            one, two = per_head(grad * base, first)
            if k == 0:
                one_sum, two_sum = jnp.sum(one, axis=0, keepdims=True), jnp.sum(two, axis=0, keepdims=True)
                sums[0] = one_sum if sums[0] is None else sums[0] + one_sum
                sums[1] = two_sum if sums[1] is None else sums[1] + two_sum
            mean = jnp.where(first, one, two) * (1.0 / hd)
            inv = jnp.where(first, invs[p, :, 2 * k : 2 * k + 1], invs[p, :, 2 * k + 1 : 2 * k + 2])
            gp[p, :, k * share : (k + 1) * share] = (factor * inv * (grad - base * mean)).astype(bf16)
        gp[p, :, 2 * share : 3 * share] = grad_v.astype(bf16)
    lane = lax.broadcasted_iota(jnp.int32, (1, share), 1)
    return jnp.where(lane == 0, sums[0], 0.0) + jnp.where(lane == 1, sums[1], 0.0)


def weight_grads(target, normed, gp, up, attended):
    split = gp.shape[2]
    qkv_part = dot(normed[0], gp[0], 0, 0) + dot(normed[1], gp[1], 0, 0)
    out_part = dot(up[0], attended[0], 0, 0) + dot(up[1], attended[1], 0, 0)
    target[:, :split] = qkv_part.astype(target.dtype)
    target[:, split:] = out_part.astype(target.dtype)


def frames_of(home):
    half = home.shape[2] // 2
    return jnp.concatenate([home[0, :, :half], home[1, :, :half]], axis=1)


def first_lanes(frames, share):
    return lax.broadcasted_iota(jnp.int32, (frames, share), 1) < share // 2


def other_kernel(
    scale, packed, in_own, in_other, act, wo_own, wo, qkv, invs, probs, attended0, attended, normed,
    bounded_out, act_part, up, gp, grads, scale_row,
    pooled,
):
    frames, width = up.shape[1:]
    share = wo.shape[0]
    summed = jnp.sum(packed[...], axis=0)
    latent = jnp.concatenate([summed[0:4], summed[4:8]], axis=1)
    cot_act = jnp.concatenate([summed[8:12], summed[12:16]], axis=1)
    shape = latent.shape
    half, offset, widths = by_level(HALF, shape), by_level(OFFSET, shape), by_level(WIDTH, shape)
    curve = jnp.tanh(latent + by_level(SHIFT, shape))
    bounded_out[...] = (curve * half - offset) / widths
    grad_latent = cot_act * (half / widths) * (1.0 - curve * curve)
    moved = pltpu.roll(grad_latent, LAG, 1)
    moved = jnp.where(lax.broadcasted_iota(jnp.int32, shape, 1) >= LAG, moved, 0.0)
    eight = jnp.concatenate([grad_latent, moved], axis=0)
    left, right = pieces(eight), pieces(act[...])
    pairs = ((0, 0), (0, 1), (1, 0), (1, 1), (0, 2), (2, 0))
    lefts = jnp.concatenate([left[i] for i, _ in pairs]).T.astype(bf16)
    rights = jnp.concatenate([right[j] for _, j in pairs]).astype(bf16)
    pooled[...] = dot(lefts, rights, 1, 0) * (1.0 / 256.0)
    half = width // 2
    for p in range(2):
        for r in range(2):
            cols = slice(r * half, (r + 1) * half)
            cot = (in_own, in_other)[p][r, :, half:].astype(f32)
            up[p, :, cols] = (cot + pooled[:, cols]).astype(bf16)
    scale_row[...] = attention_back(1, scale, up, wo, qkv, invs, probs, gp, first_lanes(frames, share))
    weight_grads(grads, normed, gp, up, attended)
    part = dot_wide(eight, frames_of(in_own), 1, 0)
    for att, w in ((attended0, wo_own), (attended, wo)):
        mixed = dot_wide(eight, att[0], 1, 0) + dot_wide(eight, att[1], 1, 0)
        part = part + dot_wide(mixed, w[...], 1, 0)
    act_part[...] = part


def own_kernel(
    scale, place, act_part, up, wo, qkv, invs, probs, attended, normed, w_own, w_other, in_own, in_other,
    gp_other, scale_other, attended1, wo_other,
    grads, small, normed_own, normed_other, enc_part,
    gp,
):
    frames, width = up.shape[1:]
    share = wo.shape[0]
    scale_own = attention_back(0, scale, up, wo, qkv, invs, probs, gp, first_lanes(frames, share))
    gain_part = None
    for p in (1, 0):
        grad = dot(gp[p], w_own[...], 1, 1) + dot(gp_other[p], w_other[...], 1, 1)
        x = frames_of((in_own, in_other)[p]).astype(f32)
        inverse = lax.rsqrt(jnp.mean(x * x, axis=-1, keepdims=True) + EPS)
        one = jnp.sum(grad * (x * inverse), axis=0, keepdims=True)
        gain_part = one if gain_part is None else gain_part + one
        if p == 0:
            normed_own[...] = grad
        else:
            normed_other[:frames] = grad.astype(bf16)
    weight_grads(grads, normed, gp, up, attended)
    for p in range(2):
        branch = dot(attended[p], wo[...], 1, 0) + dot(attended1[p], wo_other[...], 1, 0)
        if p == 0:
            enc_part[...] = frames_of(in_own).astype(f32) + branch
        else:
            normed_other[frames + 16 :] = branch.astype(bf16)
    xh, core = place[0], place[1]
    none = jnp.zeros((1, share), f32)
    for r in range(4):
        second = (xh if r < 2 else 1 - xh) == 1
        odd = (core if r % 2 == 0 else 1 - core) == 1

        def block(value):
            low = jnp.where(odd, value[:, share : 2 * share], value[:, :share])
            high = jnp.where(odd, value[:, 3 * share :], value[:, 2 * share : 3 * share])
            return jnp.where(second, high, low)

        tail = (scale_own, none, scale_other[...], none)[r]
        rows = jnp.concatenate([block(act_part[...]), block(gain_part), tail, jnp.zeros((6, share), f32)])
        if r == 1:
            normed_other[frames : frames + 16, :share] = rows.astype(bf16)
        else:
            small[r] = rows
    small[1] = jnp.zeros((16, share), f32)
    normed_other[frames : frames + 16, share:] = jnp.zeros((16, width - share), bf16)


def finish_kernel(in_own, gain, grad_own, grad_got, up, enc_part, out):
    x = frames_of(in_own).astype(f32)
    frames, width = x.shape
    inverse = lax.rsqrt(jnp.mean(x * x, axis=-1, keepdims=True) + EPS)
    scaled = gain[...] * (grad_own[...] + grad_got[:frames].astype(f32))
    row_dot = jnp.mean(scaled * x, axis=-1, keepdims=True)
    grad = inverse * scaled - x * (inverse * inverse * inverse * row_dot)
    out[:, :width] = (enc_part[...] + grad_got[frames + 16 :].astype(f32)).astype(bf16)
    out[:, width : 2 * width] = (up[0].astype(f32) + grad).astype(bf16)


VMEM = pl.BlockSpec(memory_space=pltpu.VMEM)
SMEM = pl.BlockSpec(memory_space=pltpu.SMEM)


def call(kernel, scalars, arrays, outs, flops, scratch=()):
    return pl.pallas_call(
        kernel,
        out_shape=[jax.ShapeDtypeStruct(s, d) for s, d in outs],
        in_specs=[SMEM] * len(scalars) + [VMEM] * len(arrays),
        out_specs=[VMEM] * len(outs),
        scratch_shapes=scratch,
        compiler_params=pltpu.CompilerParams(vmem_limit_bytes=60 * 1024 * 1024),
        cost_estimate=pl.CostEstimate(flops=flops, bytes_accessed=flops // 1000, transcendentals=0),
    )(*scalars, *arrays)


def local(
    frames_in,
    norm_gain,
    w_qkv,
    qk_scale,
    w_out,
    w_act,
    action_codes,
    episode_ids,
    cotangent,
    action_cotangent,
):
    fl, patches, width = frames_in.shape
    share = cotangent.shape[2]
    n_tm = lax.axis_size("xl") * lax.axis_size("y") * lax.axis_size("z")
    n_yz = lax.axis_size("y") * lax.axis_size("z")
    frames = fl * n_tm
    group = patches // 4
    tokens = frames * patches
    hd = 64
    xl, xh, core = lax.axis_index("xl"), lax.axis_index("xh"), lax.axis_index("core")
    block = xh * 2 + core
    tm = lax.axis_index(TM)
    gain = norm_gain.reshape(1, width)

    few = jnp.concatenate(
        [w_act.transpose(0, 2, 1).reshape(8, share), jnp.pad(qk_scale[None], ((0, 7), (0, share - 2)))]
    )
    few_got = swap(few, "core")
    few = ordered(few, few_got, core, 0)

    cot = cotangent.reshape(fl, 2, 2, group, share)
    cot = ordered(pick(cot, core, 2), swap(pick(cot, 1 - core, 2), "core"), core, 3)
    sent = pick(frames_in.reshape(fl, 2, 2, group, width), core, 2)
    sent = lax.dynamic_slice_in_dim(sent, xh * 2 * share, 2 * share, 3)
    sent = jnp.concatenate([sent, cot.reshape(fl, 2, group, 2 * share)], axis=-1)
    sent = sent.transpose(1, 2, 0, 3).reshape(2 * n_tm, fl, width)
    in_own = lax.all_to_all(sent, ("xh",) + TM, 0, 0, tiled=True).reshape(2, frames, width)
    in_other = swap(in_own, "core")

    w_own = w_qkv.reshape(width, 3 * share)
    w_other = swap(w_own, "xh")
    wo_other = swap(after(w_out, w_other), "xh")
    place = jnp.stack([xh, core]).astype(jnp.int32)
    few_other = swap(few, "xh")
    act = ordered(few, few_other, xh, 0).reshape(4, 16, share)[:, :8]
    act = act.transpose(1, 0, 2).reshape(8, width)
    act_own = dot(act, w_out.astype(f32), 1, 1, precision=HIGHEST)
    act_other = swap(act_own, "xh")
    scale = jnp.concatenate([qk_scale, pick(few_other, core, 0)[8, :2]])

    ids_row, ids_col = episode_ids[None], episode_ids[:, None]
    (
        normed, qkv0, qkv1, invs0, invs1, probs0, probs1, attended0, attended1, part8
    ) = call(
        forward_kernel,
        (scale,),
        (in_own, in_other, gain, w_own, w_other, ids_row, ids_col, act, act_own, act_other),
        (
            ((2, frames, width), bf16),
            ((2, 3, frames, share), bf16),
            ((2, 3, frames, share), bf16),
            ((2, frames, 4), f32),
            ((2, frames, 4), f32),
            ((2, 2, frames, frames), f32),
            ((2, 2, frames, frames), f32),
            ((2, frames, share), bf16),
            ((2, frames, share), bf16),
            ((8, frames // 2), f32),
        ),
        FORWARD_FLOPS,
    )

    ac_t = jnp.broadcast_to(action_cotangent.T[:, None], (4, n_tm, fl)).reshape(4, frames)
    ac_t = jnp.where(jnp.arange(frames)[None] // fl == tm, ac_t, 0.0)
    ac8 = jnp.concatenate([ac_t[:, : frames // 2], ac_t[:, frames // 2 :]])
    part8 = part8 + swap(part8, "core")
    packed = jnp.concatenate([part8, ac8])
    from_xh = swap(part8, "xh")
    from_xl = swap(packed, "xl")
    from_both = lax.ppermute(part8, ("xl", "xh"), [(0, 3), (1, 2), (2, 1), (3, 0)])
    far = jnp.concatenate([from_xh + from_both, jnp.zeros_like(ac8)])
    packed = (packed + from_xl) + far
    packed = jnp.broadcast_to(packed[None], (n_yz, 16, frames // 2))
    packed = lax.all_to_all(packed, YZ, 0, 0, tiled=True)

    bounded, act_part, up, gp_other, grads_other, scale_other = call(
        other_kernel,
        (scale,),
        (
            packed, in_own, in_other, act, w_out, wo_other, qkv1, invs1, probs1, attended0, attended1, normed,
        ),
        (
            ((4, frames), f32),
            ((8, width), f32),
            ((2, frames, width), bf16),
            ((2, frames, 3 * share), bf16),
            ((width, 4 * share), bf16),
            ((1, share), f32),
        ),
        BACKWARD_FLOPS,
        scratch=[pltpu.VMEM((frames, width), f32)],
    )
    grads_got = swap(grads_other, "xh")
    grads_own, small, normed_own, normed_other, enc_part = call(
        own_kernel,
        (scale, place),
        (
            act_part, up, w_out, qkv0, invs0, probs0, attended0, normed, w_own, w_other, in_own, in_other,
            gp_other, scale_other, attended1, wo_other,
        ),
        (
            ((width, 4 * share), f32),
            ((4, 16, share), f32),
            ((frames, width), f32),
            ((2 * frames + 16, width), bf16),
            ((frames, width), f32),
        ),
        BACKWARD_FLOPS,
        scratch=[pltpu.VMEM((2, frames, 3 * share), bf16)],
    )

    normed_got = swap(normed_other, "core")
    (both_out,) = call(
        finish_kernel,
        (),
        (in_own, gain, normed_own, normed_got, up, enc_part),
        (((frames, 2 * width), bf16),),
        10 * frames * width,
    )
    far = lax.ppermute(small[3], ("xh", "core"), [(0, 3), (1, 2), (2, 1), (3, 0)])
    small = (small[0] + normed_got[frames : frames + 16, :share].astype(f32)) + (swap(small[2], "xh") + far)
    small = jnp.pad(small.astype(bf16), ((0, frames - 16), (0, 0)))
    grads = (grads_own + grads_got.astype(f32)).astype(bf16)
    both_out = jnp.concatenate([both_out, grads[:frames], grads[frames:], small], axis=1)
    home = lax.all_to_all(both_out.reshape(n_tm, fl, 4 * width + share), TM, 0, 0, tiled=True)
    summed = jnp.sum(home[:, :, 2 * width :].astype(f32), axis=0).astype(bf16)
    copies = jnp.broadcast_to(summed[None], (n_tm, *summed.shape))
    summed = lax.all_to_all(copies, TM, 0, 0, tiled=True).reshape(frames, 2 * width + share)
    home = after(home[:, :, : 2 * width], copies)
    home = home.reshape(group, fl, 2, 2, 2, share)
    got = swap(pick(home, 1 - xh, 3), "xh")
    home = ordered(pick(home, xh, 3), got, xh, 0)
    got = swap(pick(home, 1 - core, 4), "core")
    home = ordered(pick(home, core, 4), got, core, 1)
    home = home.transpose(4, 3, 0, 1, 2, 5).reshape(2, fl, patches, share)
    encoded, grad_frames = home[0], home[1]

    half_level, offsets, widths = (np.array(v, np.float32)[:, None] for v in (HALF, OFFSET, WIDTH))
    bases = jnp.array([1, 8, 40, 200], dtype=jnp.int32)[:, None]
    radices = jnp.array([8, 5, 5, 5], dtype=jnp.int32)[:, None]
    digits = action_codes[None, :] // bases % radices
    bounded_own = lax.dynamic_slice_in_dim(bounded, tm * fl, fl, 1)
    quant_gap = ((digits.astype(f32) - widths) / widths - bounded_own).T

    both = jnp.concatenate([summed[:, :width], summed[:, width : 2 * width]]).astype(f32)
    norm_factor = 1.0 / math.sqrt(tokens)
    grad_qkv = both[:, : 3 * share].reshape(width, 3, share) * norm_factor
    grad_out = both[:, 3 * share : 4 * share].T * norm_factor
    small = summed[:16, 2 * width :].astype(f32)
    grad_act = small[:8].reshape(2, 4, share).transpose(0, 2, 1) * (1.0 / math.sqrt(frames) / patches)
    grad_gain = small[8] * norm_factor
    grad_qk_scale = small[9, :2] * (norm_factor / math.sqrt(hd))
    return (encoded, quant_gap, grad_frames, grad_gain, grad_qkv, grad_qk_scale, grad_out, grad_act)


def solution(mesh):
    fine = Mesh(mesh.devices.reshape(2, 4, 8, 2, 2), ("xl", "y", "z", "xh", "core"))
    head = ("xh", "core")
    in_specs = (
        P(TM, None, None),
        P(),
        P(None, None, head),
        P(head),
        P(head, None),
        P(None, head, None),
        P(TM),
        P(),
        P(TM, None, head),
        P(TM, None),
    )
    out_specs = (
        P(TM, None, head),
        P(TM, None),
        P(TM, None, head),
        P(head),
        P(None, None, head),
        P(head),
        P(head, None),
        P(None, head, None),
    )
    return jax.shard_map(local, mesh=fine, in_specs=in_specs, out_specs=out_specs, check_vma=False)
```

```python
import math

import jax
import jax.numpy as jnp
import numpy as np
from jax import lax
from jax.experimental import pallas as pl
from jax.experimental.pallas import tpu as pltpu
from jax.sharding import Mesh
from jax.sharding import PartitionSpec as P

LAG = 16
EPS = 1e-06
HIGHEST = lax.Precision.HIGHEST
TM = ("xl", "y", "z")
YZ = ("y", "z")
bf16 = jnp.bfloat16
f32 = jnp.float32
FORWARD_FLOPS = 1_000
BACKWARD_FLOPS = 5_000_000_000


def swap(value, axis):
    return lax.ppermute(value, axis, [(0, 1), (1, 0)])


def ordered(own, other, index, axis):
    first = jnp.where(index == 0, own, other)
    second = jnp.where(index == 0, other, own)
    return jnp.stack([first, second], axis=axis)


def pick(value, index, axis):
    return lax.dynamic_index_in_dim(value, index, axis, keepdims=False)


def after(value, *earlier):
    return lax.optimization_barrier((value, *earlier))[0]


HALF = [(n - 1.0) * (1.0 - 0.001) / 2.0 for n in (8.0, 5.0, 5.0, 5.0)]
OFFSET = [0.5, 0.0, 0.0, 0.0]
WIDTH = [4.0, 2.0, 2.0, 2.0]
SHIFT = [0.5 * math.log((a + b) / (a - b)) for a, b in zip(HALF, OFFSET)]


def by_level(values, shape):
    row = lax.broadcasted_iota(jnp.int32, shape, 0)
    return jnp.where(row == 0, values[0], values[1]).astype(f32)


def dot(a, b, ca, cb, **kw):
    return lax.dot_general(a, b, (((ca,), (cb,)), ((), ())), preferred_element_type=f32, **kw)


def pieces(values):
    high = values.astype(bf16).astype(f32)
    middle = (values - high).astype(bf16).astype(f32)
    return high, middle, (values - high - middle).astype(bf16).astype(f32)


def dot_wide(few, many, ca, cb):
    rows = few.shape[0]
    out = dot(jnp.concatenate(pieces(few)).astype(bf16), many, ca, cb)
    return out[:rows] + (out[rows : 2 * rows] + out[2 * rows :])


def per_head(values, first):
    one = jnp.sum(jnp.where(first, values, 0.0), axis=-1, keepdims=True)
    two = jnp.sum(jnp.where(first, 0.0, values), axis=-1, keepdims=True)
    return one, two


def attention_forward(b, scale, normed, w, ids_row, ids_col, qkv, invs, probs, attended):
    frames, share = qkv.shape[2:]
    hd, mid = share // 2, frames // 2
    first = first_lanes(frames, share)
    t = lax.broadcasted_iota(jnp.int32, (frames, frames), 0)
    u = lax.broadcasted_iota(jnp.int32, (frames, frames), 1)
    visible = jnp.logical_and(ids_col[...] == ids_row[...], u <= t)
    for p in range(2):
        raw = dot(normed[p], w[...], 1, 0)
        parts = []
        for k in range(2):
            one = raw[:, k * share : (k + 1) * share]
            sums = per_head(one * one, first)
            inv0 = lax.rsqrt(sums[0] * (1.0 / hd) + EPS)
            inv1 = lax.rsqrt(sums[1] * (1.0 / hd) + EPS)
            invs[p, :, k * 2 : k * 2 + 1] = inv0
            invs[p, :, k * 2 + 1 : k * 2 + 2] = inv1
            parts.append((one * jnp.where(first, inv0, inv1)).astype(bf16))
        parts.append(raw[:, 2 * share :].astype(bf16))
        query, keys, values = parts
        for k in range(3):
            qkv[p, k] = parts[k]
        zero = jnp.zeros_like(keys)
        mixed = [None, None]
        for h in range(2):
            mask = first if h == 0 else jnp.logical_not(first)
            keys_h, values_h = jnp.where(mask, keys, zero), jnp.where(mask, values, zero)
            factor = scale[b * 2 + h] * (1.0 / math.sqrt(hd))
            for k, (rows, seen) in enumerate(((slice(0, mid), mid), (slice(mid, frames), frames))):
                dots = dot(query[rows], keys_h[:seen], 1, 1)
                weights = jnp.where(visible[rows, :seen], jnp.exp(dots * factor), 0.0)
                prob = weights * (1.0 / jnp.sum(weights, axis=-1, keepdims=True))
                probs[p, h, rows, :seen] = prob
                one = dot(prob.astype(bf16), values_h[:seen], 1, 0)
                mixed[k] = one if mixed[k] is None else mixed[k] + one
        attended[p] = jnp.concatenate(mixed).astype(bf16)


def forward_kernel(
    scale, in_own, in_other, gain, w_own, w_other, ids_row, ids_col, act, act_own, act_other,
    normed, qkv0, qkv1, invs0, invs1, probs0, probs1, attended0, attended1, part8,
):
    frames = in_own.shape[1]
    for p in range(2):
        x = frames_of((in_own, in_other)[p]).astype(f32)
        inverse = lax.rsqrt(jnp.mean(x * x, axis=-1, keepdims=True) + EPS)
        normed[p] = (x * inverse * gain[...]).astype(bf16)
    attention_forward(0, scale, normed, w_own, ids_row, ids_col, qkv0, invs0, probs0, attended0)
    attention_forward(1, scale, normed, w_other, ids_row, ids_col, qkv1, invs1, probs1, attended1)
    terms = dot_wide(act[...], frames_of(in_own), 1, 1)
    for act_out, att in ((act_own, attended0), (act_other, attended1)):
        terms = terms + (dot_wide(act_out[...], att[0], 1, 1) + dot_wide(act_out[...], att[1], 1, 1))
    terms = terms * (1.0 / 256.0)
    moved = pltpu.roll(terms, frames - LAG, 1)
    moved = jnp.where(lax.broadcasted_iota(jnp.int32, moved.shape, 1) < frames - LAG, moved, 0.0)
    part = terms[:4] + moved[4:]
    part8[0:4] = part[:, : frames // 2]
    part8[4:8] = part[:, frames // 2 :]


def attention_back(b, scale, up, wo, qkv, invs, probs, gp, first):
    share, frames = wo.shape[0], up.shape[1]
    hd, mid = share // 2, frames // 2
    sums = [None, None]
    factor = jnp.where(
        first[:1], scale[b * 2] * (1.0 / math.sqrt(hd)), scale[b * 2 + 1] * (1.0 / math.sqrt(hd))
    )
    for p in range(2):
        query, keys, values = qkv[p, 0], qkv[p, 1], qkv[p, 2]
        zero = jnp.zeros_like(keys)
        grad_att = dot(up[p], wo[...], 1, 1).astype(bf16)
        grad_q, low, high = [None, None], [None, None], [None, None]

        def add(old, new):
            return new if old is None else old + new

        for h in range(2):
            mask = first if h == 0 else jnp.logical_not(first)
            query_h, keys_h = jnp.where(mask, query, zero), jnp.where(mask, keys, zero)
            values_h, grad_h = jnp.where(mask, values, zero), jnp.where(mask, grad_att, zero)
            for k, (rows, seen) in enumerate(((slice(0, mid), mid), (slice(mid, frames), frames))):
                grad_probs = dot(grad_att[rows], values_h[:seen], 1, 1)
                prob = probs[p, h, rows, :seen]
                inner = jnp.sum(grad_probs * prob, axis=-1, keepdims=True)
                grad_scores = (prob * (grad_probs - inner)).astype(bf16)
                grad_q[k] = add(grad_q[k], dot(grad_scores, keys_h[:seen], 1, 0))
                target = (low, high)[k]
                target[0] = add(target[0], dot(grad_scores, query_h[rows], 0, 0))
                target[1] = add(target[1], dot(prob.astype(bf16), grad_h[rows], 0, 0))
        grad_q = jnp.concatenate(grad_q)
        grad_k, grad_v = (jnp.concatenate([low[j] + high[j][:mid], high[j][mid:]]) for j in range(2))
        for k in range(2):
            grad, base = ((grad_q, query), (grad_k, keys))[k]
            base = base.astype(f32)
            one, two = per_head(grad * base, first)
            if k == 0:
                one_sum, two_sum = jnp.sum(one, axis=0, keepdims=True), jnp.sum(two, axis=0, keepdims=True)
                sums[0] = one_sum if sums[0] is None else sums[0] + one_sum
                sums[1] = two_sum if sums[1] is None else sums[1] + two_sum
            mean = jnp.where(first, one, two) * (1.0 / hd)
            inv = jnp.where(first, invs[p, :, 2 * k : 2 * k + 1], invs[p, :, 2 * k + 1 : 2 * k + 2])
            gp[p, :, k * share : (k + 1) * share] = (factor * inv * (grad - base * mean)).astype(bf16)
        gp[p, :, 2 * share : 3 * share] = grad_v.astype(bf16)
    lane = lax.broadcasted_iota(jnp.int32, (1, share), 1)
    return jnp.where(lane == 0, sums[0], 0.0) + jnp.where(lane == 1, sums[1], 0.0)


def prepare_kernel(normed, attended0, attended1, normed_t, attended0_t, attended1_t):
    for p in range(2):
        normed_t[p] = normed[p].T
        attended0_t[p] = attended0[p].T
        attended1_t[p] = attended1[p].T


def weight_grads(target, normed_t, gp, up, attended_t):
    split = gp.shape[2]
    half, share = normed_t.shape[1] // 2, attended_t.shape[1]
    qkv_part = dot(normed_t[0], gp[0], 1, 0) + dot(normed_t[1], gp[1], 1, 0)
    out_part = dot(attended_t[0], up[0], 1, 0) + dot(attended_t[1], up[1], 1, 0)
    for k in range(2):
        target[:, k * split : (k + 1) * split] = qkv_part[k * half : (k + 1) * half].astype(target.dtype)
        target[k * share : (k + 1) * share, 2 * split :] = out_part[:, k * half : (k + 1) * half].astype(target.dtype)


def frames_of(home):
    half = home.shape[2] // 2
    return jnp.concatenate([home[0, :, :half], home[1, :, :half]], axis=1)


def first_lanes(frames, share):
    return lax.broadcasted_iota(jnp.int32, (frames, share), 1) < share // 2


def other_kernel(
    scale, packed, in_own, in_other, act, wo_own, wo, qkv, invs, probs, attended0, attended, normed_t, attended_t,
    bounded_out, act_part, up, gp, grads, scale_row,
    pooled,
):
    frames, width = up.shape[1:]
    share = wo.shape[0]
    summed = jnp.sum(packed[...], axis=0)
    latent = jnp.concatenate([summed[0:4], summed[4:8]], axis=1)
    cot_act = jnp.concatenate([summed[8:12], summed[12:16]], axis=1)
    shape = latent.shape
    half, offset, widths = by_level(HALF, shape), by_level(OFFSET, shape), by_level(WIDTH, shape)
    curve = jnp.tanh(latent + by_level(SHIFT, shape))
    bounded_out[...] = (curve * half - offset) / widths
    grad_latent = cot_act * (half / widths) * (1.0 - curve * curve)
    moved = pltpu.roll(grad_latent, LAG, 1)
    moved = jnp.where(lax.broadcasted_iota(jnp.int32, shape, 1) >= LAG, moved, 0.0)
    eight = jnp.concatenate([grad_latent, moved], axis=0)
    left, right = pieces(eight), pieces(act[...])
    pairs = ((0, 0), (0, 1), (1, 0), (1, 1), (0, 2), (2, 0))
    lefts = jnp.concatenate([left[i] for i, _ in pairs]).T.astype(bf16)
    rights = jnp.concatenate([right[j] for _, j in pairs]).astype(bf16)
    pooled[...] = dot(lefts, rights, 1, 0) * (1.0 / 256.0)
    half = width // 2
    for p in range(2):
        for r in range(2):
            cols = slice(r * half, (r + 1) * half)
            cot = (in_own, in_other)[p][r, :, half:].astype(f32)
            up[p, :, cols] = (cot + pooled[:, cols]).astype(bf16)
    scale_row[...] = attention_back(1, scale, up, wo, qkv, invs, probs, gp, first_lanes(frames, share))
    weight_grads(grads, normed_t, gp, up, attended_t)
    part = dot_wide(eight, frames_of(in_own), 1, 0)
    for att, w in ((attended0, wo_own), (attended, wo)):
        mixed = dot_wide(eight, att[0], 1, 0) + dot_wide(eight, att[1], 1, 0)
        part = part + dot_wide(mixed, w[...], 1, 0)
    act_part[...] = part


def own_kernel(
    scale, place, act_part, up, wo, qkv, invs, probs, attended, normed_t, attended_t, w_own, w_other, in_own, in_other,
    gp_other, scale_other, attended1, wo_other,
    grads, small, small2, small3, normed_own, normed_other, enc_part,
    gp,
):
    frames, width = up.shape[1:]
    share = wo.shape[0]
    scale_own = attention_back(0, scale, up, wo, qkv, invs, probs, gp, first_lanes(frames, share))
    gain_part = None
    for p in (1, 0):
        grad = dot(gp[p], w_own[...], 1, 1) + dot(gp_other[p], w_other[...], 1, 1)
        x = frames_of((in_own, in_other)[p]).astype(f32)
        inverse = lax.rsqrt(jnp.mean(x * x, axis=-1, keepdims=True) + EPS)
        one = jnp.sum(grad * (x * inverse), axis=0, keepdims=True)
        gain_part = one if gain_part is None else gain_part + one
        if p == 0:
            normed_own[...] = grad
        else:
            normed_other[:frames] = grad.astype(bf16)
    weight_grads(grads, normed_t, gp, up, attended_t)
    for p in range(2):
        branch = dot(attended[p], wo[...], 1, 0) + dot(attended1[p], wo_other[...], 1, 0)
        if p == 0:
            enc_part[...] = frames_of(in_own).astype(f32) + branch
        else:
            normed_other[frames + 16 :] = branch.astype(bf16)
    xh, core = place[0], place[1]
    none = jnp.zeros((1, share), f32)
    for r in range(4):
        second = (xh if r < 2 else 1 - xh) == 1
        odd = (core if r % 2 == 0 else 1 - core) == 1

        def block(value):
            low = jnp.where(odd, value[:, share : 2 * share], value[:, :share])
            high = jnp.where(odd, value[:, 3 * share :], value[:, 2 * share : 3 * share])
            return jnp.where(second, high, low)

        tail = (scale_own, none, scale_other[...], none)[r]
        rows = jnp.concatenate([block(act_part[...]), block(gain_part), tail, jnp.zeros((6, share), f32)])
        if r == 1:
            normed_other[frames : frames + 16, :share] = rows.astype(bf16)
        else:
            (small, None, small2, small3)[r][...] = rows
    normed_other[frames : frames + 16, share:] = jnp.zeros((16, width - share), bf16)


def finish_kernel(in_own, gain, grad_own, grad_got, up, enc_part, out):
    x = frames_of(in_own).astype(f32)
    frames, width = x.shape
    inverse = lax.rsqrt(jnp.mean(x * x, axis=-1, keepdims=True) + EPS)
    scaled = gain[...] * (grad_own[...] + grad_got[:frames].astype(f32))
    row_dot = jnp.mean(scaled * x, axis=-1, keepdims=True)
    grad = inverse * scaled - x * (inverse * inverse * inverse * row_dot)
    out[:, :width] = (enc_part[...] + grad_got[frames + 16 :].astype(f32)).astype(bf16)
    out[:, width : 2 * width] = (up[0].astype(f32) + grad).astype(bf16)


VMEM = pl.BlockSpec(memory_space=pltpu.VMEM)
SMEM = pl.BlockSpec(memory_space=pltpu.SMEM)


def call(kernel, scalars, arrays, outs, flops, scratch=()):
    return pl.pallas_call(
        kernel,
        out_shape=[jax.ShapeDtypeStruct(s, d) for s, d in outs],
        in_specs=[SMEM] * len(scalars) + [VMEM] * len(arrays),
        out_specs=[VMEM] * len(outs),
        scratch_shapes=scratch,
        compiler_params=pltpu.CompilerParams(vmem_limit_bytes=60 * 1024 * 1024),
        cost_estimate=pl.CostEstimate(flops=flops, bytes_accessed=flops // 1000, transcendentals=0),
    )(*scalars, *arrays)


def local(
    frames_in,
    norm_gain,
    w_qkv,
    qk_scale,
    w_out,
    w_act,
    action_codes,
    episode_ids,
    cotangent,
    action_cotangent,
):
    fl, patches, width = frames_in.shape
    share = cotangent.shape[2]
    n_tm = lax.axis_size("xl") * lax.axis_size("y") * lax.axis_size("z")
    n_yz = lax.axis_size("y") * lax.axis_size("z")
    frames = fl * n_tm
    group = patches // 4
    tokens = frames * patches
    hd = 64
    xl, xh, core = lax.axis_index("xl"), lax.axis_index("xh"), lax.axis_index("core")
    block = xh * 2 + core
    tm = lax.axis_index(TM)
    gain = norm_gain.reshape(1, width)

    few = jnp.concatenate(
        [w_act.transpose(0, 2, 1).reshape(8, share), jnp.pad(qk_scale[None], ((0, 7), (0, share - 2)))]
    )
    few_got = swap(few, "core")
    few = ordered(few, few_got, core, 0)

    cot = cotangent.reshape(fl, 2, 2, group, share)
    cot = ordered(pick(cot, core, 2), swap(pick(cot, 1 - core, 2), "core"), core, 3)
    sent = pick(frames_in.reshape(fl, 2, 2, group, width), core, 2)
    sent = lax.dynamic_slice_in_dim(sent, xh * 2 * share, 2 * share, 3)
    sent = jnp.concatenate([sent, cot.reshape(fl, 2, group, 2 * share)], axis=-1)
    sent = sent.transpose(1, 2, 0, 3).reshape(2 * n_tm, fl, width)
    in_own = lax.all_to_all(sent, ("xh",) + TM, 0, 0, tiled=True).reshape(2, frames, width)
    in_other = swap(in_own, "core")

    w_own = w_qkv.reshape(width, 3 * share)
    w_other = swap(w_own, "xh")
    wo_other = swap(after(w_out, w_other), "xh")
    place = jnp.stack([xh, core]).astype(jnp.int32)
    few_other = swap(few, "xh")
    act = ordered(few, few_other, xh, 0).reshape(4, 16, share)[:, :8]
    act = act.transpose(1, 0, 2).reshape(8, width)
    act_own = dot(act, w_out.astype(f32), 1, 1, precision=HIGHEST)
    act_other = swap(act_own, "xh")
    scale = jnp.concatenate([qk_scale, pick(few_other, core, 0)[8, :2]])

    ids_row, ids_col = episode_ids[None], episode_ids[:, None]
    (
        normed, qkv0, qkv1, invs0, invs1, probs0, probs1, attended0, attended1, part8
    ) = call(
        forward_kernel,
        (scale,),
        (in_own, in_other, gain, w_own, w_other, ids_row, ids_col, act, act_own, act_other),
        (
            ((2, frames, width), bf16),
            ((2, 3, frames, share), bf16),
            ((2, 3, frames, share), bf16),
            ((2, frames, 4), f32),
            ((2, frames, 4), f32),
            ((2, 2, frames, frames), f32),
            ((2, 2, frames, frames), f32),
            ((2, frames, share), bf16),
            ((2, frames, share), bf16),
            ((8, frames // 2), f32),
        ),
        FORWARD_FLOPS,
    )

    ac_t = jnp.broadcast_to(action_cotangent.T[:, None], (4, n_tm, fl)).reshape(4, frames)
    ac_t = jnp.where(jnp.arange(frames)[None] // fl == tm, ac_t, 0.0)
    ac8 = jnp.concatenate([ac_t[:, : frames // 2], ac_t[:, frames // 2 :]])
    part8 = part8 + swap(part8, "core")
    packed = jnp.concatenate([part8, ac8])
    from_xh = swap(part8, "xh")
    from_xl = swap(packed, "xl")
    from_both = lax.ppermute(part8, ("xl", "xh"), [(0, 3), (1, 2), (2, 1), (3, 0)])
    far = jnp.concatenate([from_xh + from_both, jnp.zeros_like(ac8)])
    sums = (packed + from_xl) + far
    packed = jnp.broadcast_to(sums[None], (n_yz, 16, frames // 2))
    packed = lax.all_to_all(packed, YZ, 0, 0, tiled=True)

    normed_t, attended0_t, attended1_t = call(
        prepare_kernel,
        (),
        (after(normed, sums), attended0, attended1),
        (((2, width, frames), bf16), ((2, share, frames), bf16), ((2, share, frames), bf16)),
        FORWARD_FLOPS,
    )
    bounded, act_part, up, gp_other, grads_other, scale_other = call(
        other_kernel,
        (scale,),
        (
            packed, in_own, in_other, act, w_out, wo_other, qkv1, invs1, probs1, attended0, attended1, normed_t, attended1_t,
        ),
        (
            ((4, frames), f32),
            ((8, width), f32),
            ((2, frames, width), bf16),
            ((2, frames, 3 * share), bf16),
            ((width // 2, 2 * width), bf16),
            ((1, share), f32),
        ),
        BACKWARD_FLOPS,
        scratch=[pltpu.VMEM((frames, width), f32)],
    )
    grads_got = swap(grads_other, "xh")
    grads_own, small, small2, small3, normed_own, normed_other, enc_part = call(
        own_kernel,
        (scale, place),
        (
            act_part, up, w_out, qkv0, invs0, probs0, attended0, normed_t, attended0_t, w_own, w_other, in_own, in_other,
            gp_other, scale_other, attended1, wo_other,
        ),
        (
            ((width // 2, 2 * width), f32),
            ((16, share), f32),
            ((16, share), f32),
            ((16, share), f32),
            ((frames, width), f32),
            ((2 * frames + 16, width), bf16),
            ((frames, width), f32),
        ),
        BACKWARD_FLOPS,
        scratch=[pltpu.VMEM((2, frames, 3 * share), bf16)],
    )

    normed_got = swap(normed_other, "core")
    (both_out,) = call(
        finish_kernel,
        (),
        (in_own, gain, normed_own, normed_got, up, enc_part),
        (((frames, 2 * width), bf16),),
        10 * frames * width,
    )
    far = lax.ppermute(small3, ("xh", "core"), [(0, 3), (1, 2), (2, 1), (3, 0)])
    small = (small + normed_got[frames : frames + 16, :share].astype(f32)) + (swap(small2, "xh") + far)
    small = jnp.pad(small.astype(bf16), ((0, frames - 16), (0, 0)))
    grads = (grads_own + grads_got.astype(f32)).astype(bf16)
    both_out = jnp.concatenate([both_out, grads, small], axis=1)
    home = lax.all_to_all(both_out.reshape(n_tm, fl, 4 * width + share), TM, 0, 0, tiled=True)
    summed = jnp.sum(home[:, :, 2 * width :].astype(f32), axis=0).astype(bf16)
    copies = jnp.broadcast_to(summed[None], (n_tm, *summed.shape))
    summed = lax.all_to_all(copies, TM, 0, 0, tiled=True).reshape(frames, 2 * width + share)
    home = after(home[:, :, : 2 * width], copies)
    home = home.reshape(group, fl, 2, 2, 2, share)

    def block_of(x_index, core_index):
        return pick(pick(home, x_index, 3), core_index, 3)

    from_core = swap(block_of(xh, 1 - core), "core")
    from_xh = swap(block_of(1 - xh, core), "xh")
    from_both = lax.ppermute(block_of(1 - xh, 1 - core), ("xh", "core"), [(0, 3), (1, 2), (2, 1), (3, 0)])
    near = ordered(block_of(xh, core), from_core, core, 0)
    home = ordered(near, ordered(from_xh, from_both, core, 0), xh, 0)
    home = home.transpose(4, 3, 0, 1, 2, 5).reshape(2, fl, patches, share)
    encoded, grad_frames = home[0], home[1]

    half_level, offsets, widths = (np.array(v, np.float32)[:, None] for v in (HALF, OFFSET, WIDTH))
    bases = jnp.array([1, 8, 40, 200], dtype=jnp.int32)[:, None]
    radices = jnp.array([8, 5, 5, 5], dtype=jnp.int32)[:, None]
    digits = action_codes[None, :] // bases % radices
    bounded_own = lax.dynamic_slice_in_dim(bounded, tm * fl, fl, 1)
    quant_gap = ((digits.astype(f32) - widths) / widths - bounded_own).T

    norm_factor = 1.0 / math.sqrt(tokens)
    qkv_halves = jnp.concatenate([summed[:, : 3 * share], summed[:, 3 * share : 6 * share]])
    grad_qkv = qkv_halves.astype(f32).reshape(width, 3, share) * norm_factor
    out_halves = [summed[k * share : (k + 1) * share, 6 * share : 2 * width] for k in range(2)]
    grad_out = jnp.concatenate(out_halves, axis=1).astype(f32) * norm_factor
    small = summed[:16, 2 * width :].astype(f32)
    grad_act = small[:8].reshape(2, 4, share).transpose(0, 2, 1) * (1.0 / math.sqrt(frames) / patches)
    grad_gain = small[8] * norm_factor
    grad_qk_scale = small[9, :2] * (norm_factor / math.sqrt(hd))
    return (encoded, quant_gap, grad_frames, grad_gain, grad_qkv, grad_qk_scale, grad_out, grad_act)


def solution(mesh):
    fine = Mesh(mesh.devices.reshape(2, 4, 8, 2, 2), ("xl", "y", "z", "xh", "core"))
    head = ("xh", "core")
    in_specs = (
        P(TM, None, None),
        P(),
        P(None, None, head),
        P(head),
        P(head, None),
        P(None, head, None),
        P(TM),
        P(),
        P(TM, None, head),
        P(TM, None),
    )
    out_specs = (
        P(TM, None, head),
        P(TM, None),
        P(TM, None, head),
        P(head),
        P(None, None, head),
        P(head),
        P(head, None),
        P(None, head, None),
    )
    return jax.shard_map(local, mesh=fine, in_specs=in_specs, out_specs=out_specs, check_vma=False)
```

```python
import math

import jax
import jax.numpy as jnp
import numpy as np
from jax import lax
from jax.experimental import pallas as pl
from jax.experimental.pallas import tpu as pltpu
from jax.sharding import Mesh
from jax.sharding import PartitionSpec as P

LAG = 16
EPS = 1e-06
HIGHEST = lax.Precision.HIGHEST
TM = ("xl", "y", "z")
YZ = ("y", "z")
bf16 = jnp.bfloat16
f32 = jnp.float32
FORWARD_FLOPS = 1_000
BACKWARD_FLOPS = 5_000_000_000


def swap(value, axis):
    return lax.ppermute(value, axis, [(0, 1), (1, 0)])


def ordered(own, other, index, axis):
    first = jnp.where(index == 0, own, other)
    second = jnp.where(index == 0, other, own)
    return jnp.stack([first, second], axis=axis)


def pick(value, index, axis):
    return lax.dynamic_index_in_dim(value, index, axis, keepdims=False)


def after(value, *earlier):
    return lax.optimization_barrier((value, *earlier))[0]


HALF = [(n - 1.0) * (1.0 - 0.001) / 2.0 for n in (8.0, 5.0, 5.0, 5.0)]
OFFSET = [0.5, 0.0, 0.0, 0.0]
WIDTH = [4.0, 2.0, 2.0, 2.0]
SHIFT = [0.5 * math.log((a + b) / (a - b)) for a, b in zip(HALF, OFFSET)]


def by_level(values, shape):
    row = lax.broadcasted_iota(jnp.int32, shape, 0)
    return jnp.where(row == 0, values[0], values[1]).astype(f32)


def dot(a, b, ca, cb, **kw):
    return lax.dot_general(a, b, (((ca,), (cb,)), ((), ())), preferred_element_type=f32, **kw)


def pieces(values):
    high = values.astype(bf16).astype(f32)
    middle = (values - high).astype(bf16).astype(f32)
    return high, middle, (values - high - middle).astype(bf16).astype(f32)


def dot_wide(few, many, ca, cb):
    rows = few.shape[0]
    out = dot(jnp.concatenate(pieces(few)).astype(bf16), many, ca, cb)
    return out[:rows] + (out[rows : 2 * rows] + out[2 * rows :])


def per_head(values, first):
    one = jnp.sum(jnp.where(first, values, 0.0), axis=-1, keepdims=True)
    two = jnp.sum(jnp.where(first, 0.0, values), axis=-1, keepdims=True)
    return one, two


def attention_forward(b, scale, normed, w, ids_row, ids_col, qkv, invs, probs, attended):
    frames, share = qkv.shape[2:]
    hd, mid = share // 2, frames // 2
    first = first_lanes(frames, share)
    t = lax.broadcasted_iota(jnp.int32, (frames, frames), 0)
    u = lax.broadcasted_iota(jnp.int32, (frames, frames), 1)
    visible = jnp.logical_and(ids_col[...] == ids_row[...], u <= t)
    for p in range(2):
        raw = dot(normed[p], w[...], 1, 0)
        parts = []
        for k in range(2):
            one = raw[:, k * share : (k + 1) * share]
            sums = per_head(one * one, first)
            inv0 = lax.rsqrt(sums[0] * (1.0 / hd) + EPS)
            inv1 = lax.rsqrt(sums[1] * (1.0 / hd) + EPS)
            invs[p, :, k * 2 : k * 2 + 1] = inv0
            invs[p, :, k * 2 + 1 : k * 2 + 2] = inv1
            parts.append((one * jnp.where(first, inv0, inv1)).astype(bf16))
        parts.append(raw[:, 2 * share :].astype(bf16))
        query, keys, values = parts
        for k in range(3):
            qkv[p, k] = parts[k]
        zero = jnp.zeros_like(keys)
        mixed = [None, None]
        for h in range(2):
            mask = first if h == 0 else jnp.logical_not(first)
            keys_h, values_h = jnp.where(mask, keys, zero), jnp.where(mask, values, zero)
            factor = scale[b * 2 + h] * (1.0 / math.sqrt(hd))
            for k, (rows, seen) in enumerate(((slice(0, mid), mid), (slice(mid, frames), frames))):
                dots = dot(query[rows], keys_h[:seen], 1, 1)
                weights = jnp.where(visible[rows, :seen], jnp.exp(dots * factor), 0.0)
                prob = weights * (1.0 / jnp.sum(weights, axis=-1, keepdims=True))
                probs[p, h, rows, :seen] = prob
                one = dot(prob.astype(bf16), values_h[:seen], 1, 0)
                mixed[k] = one if mixed[k] is None else mixed[k] + one
        attended[p] = jnp.concatenate(mixed).astype(bf16)


def forward_kernel(
    scale, in_own, in_other, gain, w_own, w_other, ids_row, ids_col, act, act_own, act_other,
    normed, qkv0, qkv1, invs0, invs1, probs0, probs1, attended0, attended1, part8,
):
    frames = in_own.shape[1]
    for p in range(2):
        x = frames_of((in_own, in_other)[p]).astype(f32)
        inverse = lax.rsqrt(jnp.mean(x * x, axis=-1, keepdims=True) + EPS)
        normed[p] = (x * inverse * gain[...]).astype(bf16)
    attention_forward(0, scale, normed, w_own, ids_row, ids_col, qkv0, invs0, probs0, attended0)
    attention_forward(1, scale, normed, w_other, ids_row, ids_col, qkv1, invs1, probs1, attended1)
    terms = dot_wide(act[...], frames_of(in_own), 1, 1)
    for act_out, att in ((act_own, attended0), (act_other, attended1)):
        terms = terms + (dot_wide(act_out[...], att[0], 1, 1) + dot_wide(act_out[...], att[1], 1, 1))
    terms = terms * (1.0 / 256.0)
    moved = pltpu.roll(terms, frames - LAG, 1)
    moved = jnp.where(lax.broadcasted_iota(jnp.int32, moved.shape, 1) < frames - LAG, moved, 0.0)
    part = terms[:4] + moved[4:]
    part8[0:4] = part[:, : frames // 2]
    part8[4:8] = part[:, frames // 2 :]


def attention_back(b, scale, up, wo, qkv, invs, probs, gp, first):
    share, frames = wo.shape[0], up.shape[1]
    hd, mid = share // 2, frames // 2
    sums = [None, None]
    factor = jnp.where(
        first[:1], scale[b * 2] * (1.0 / math.sqrt(hd)), scale[b * 2 + 1] * (1.0 / math.sqrt(hd))
    )
    for p in range(2):
        query, keys, values = qkv[p, 0], qkv[p, 1], qkv[p, 2]
        zero = jnp.zeros_like(keys)
        grad_att = dot(up[p], wo[...], 1, 1).astype(bf16)
        grad_q, low, high = [None, None], [None, None], [None, None]

        def add(old, new):
            return new if old is None else old + new

        for h in range(2):
            mask = first if h == 0 else jnp.logical_not(first)
            query_h, keys_h = jnp.where(mask, query, zero), jnp.where(mask, keys, zero)
            values_h, grad_h = jnp.where(mask, values, zero), jnp.where(mask, grad_att, zero)
            for k, (rows, seen) in enumerate(((slice(0, mid), mid), (slice(mid, frames), frames))):
                grad_probs = dot(grad_att[rows], values_h[:seen], 1, 1)
                prob = probs[p, h, rows, :seen]
                inner = jnp.sum(grad_probs * prob, axis=-1, keepdims=True)
                grad_scores = (prob * (grad_probs - inner)).astype(bf16)
                grad_q[k] = add(grad_q[k], dot(grad_scores, keys_h[:seen], 1, 0))
                target = (low, high)[k]
                target[0] = add(target[0], dot(grad_scores, query_h[rows], 0, 0))
                target[1] = add(target[1], dot(prob.astype(bf16), grad_h[rows], 0, 0))
        grad_q = jnp.concatenate(grad_q)
        grad_k, grad_v = (jnp.concatenate([low[j] + high[j][:mid], high[j][mid:]]) for j in range(2))
        for k in range(2):
            grad, base = ((grad_q, query), (grad_k, keys))[k]
            base = base.astype(f32)
            one, two = per_head(grad * base, first)
            if k == 0:
                one_sum, two_sum = jnp.sum(one, axis=0, keepdims=True), jnp.sum(two, axis=0, keepdims=True)
                sums[0] = one_sum if sums[0] is None else sums[0] + one_sum
                sums[1] = two_sum if sums[1] is None else sums[1] + two_sum
            mean = jnp.where(first, one, two) * (1.0 / hd)
            inv = jnp.where(first, invs[p, :, 2 * k : 2 * k + 1], invs[p, :, 2 * k + 1 : 2 * k + 2])
            gp[p, :, k * share : (k + 1) * share] = (factor * inv * (grad - base * mean)).astype(bf16)
        gp[p, :, 2 * share : 3 * share] = grad_v.astype(bf16)
    lane = lax.broadcasted_iota(jnp.int32, (1, share), 1)
    return jnp.where(lane == 0, sums[0], 0.0) + jnp.where(lane == 1, sums[1], 0.0)


def prepare_kernel(normed, attended0, attended1, normed_t, attended0_t, attended1_t):
    for p in range(2):
        normed_t[p] = normed[p].T
        attended0_t[p] = attended0[p].T
        attended1_t[p] = attended1[p].T


def weight_grads(target, normed_t, gp, up, attended_t):
    split = gp.shape[2]
    half, share = normed_t.shape[1] // 2, attended_t.shape[1]
    qkv_part = dot(normed_t[0], gp[0], 1, 0) + dot(normed_t[1], gp[1], 1, 0)
    out_part = dot(attended_t[0], up[0], 1, 0) + dot(attended_t[1], up[1], 1, 0)
    for k in range(2):
        target[:, k * split : (k + 1) * split] = qkv_part[k * half : (k + 1) * half].astype(target.dtype)
        target[k * share : (k + 1) * share, 2 * split :] = out_part[:, k * half : (k + 1) * half].astype(target.dtype)


def frames_of(home):
    half = home.shape[2] // 2
    return jnp.concatenate([home[0, :, :half], home[1, :, :half]], axis=1)


def first_lanes(frames, share):
    return lax.broadcasted_iota(jnp.int32, (frames, share), 1) < share // 2


def other_kernel(
    scale, packed, in_own, in_other, act, wo_own, wo, qkv, invs, probs, attended0, attended, normed_t, attended_t,
    bounded_out, act_part, up, gp, grads, scale_row,
    pooled,
):
    frames, width = up.shape[1:]
    share = wo.shape[0]
    summed = jnp.sum(packed[...], axis=0)
    latent = jnp.concatenate([summed[0:4], summed[4:8]], axis=1)
    cot_act = jnp.concatenate([summed[8:12], summed[12:16]], axis=1)
    shape = latent.shape
    half, offset, widths = by_level(HALF, shape), by_level(OFFSET, shape), by_level(WIDTH, shape)
    curve = jnp.tanh(latent + by_level(SHIFT, shape))
    bounded_out[...] = (curve * half - offset) / widths
    grad_latent = cot_act * (half / widths) * (1.0 - curve * curve)
    moved = pltpu.roll(grad_latent, LAG, 1)
    moved = jnp.where(lax.broadcasted_iota(jnp.int32, shape, 1) >= LAG, moved, 0.0)
    eight = jnp.concatenate([grad_latent, moved], axis=0)
    left, right = pieces(eight), pieces(act[...])
    pairs = ((0, 0), (0, 1), (1, 0), (1, 1), (0, 2), (2, 0))
    lefts = jnp.concatenate([left[i] for i, _ in pairs]).T.astype(bf16)
    rights = jnp.concatenate([right[j] for _, j in pairs]).astype(bf16)
    pooled[...] = dot(lefts, rights, 1, 0) * (1.0 / 256.0)
    half = width // 2
    for p in range(2):
        for r in range(2):
            cols = slice(r * half, (r + 1) * half)
            cot = (in_own, in_other)[p][r, :, half:].astype(f32)
            up[p, :, cols] = (cot + pooled[:, cols]).astype(bf16)
    scale_row[...] = attention_back(1, scale, up, wo, qkv, invs, probs, gp, first_lanes(frames, share))
    weight_grads(grads, normed_t, gp, up, attended_t)
    part = dot_wide(eight, frames_of(in_own), 1, 0)
    for att, w in ((attended0, wo_own), (attended, wo)):
        mixed = dot_wide(eight, att[0], 1, 0) + dot_wide(eight, att[1], 1, 0)
        part = part + dot_wide(mixed, w[...], 1, 0)
    act_part[...] = part


def own_kernel(
    scale, place, act_part, up, wo, qkv, invs, probs, attended, normed_t, attended_t, w_own, w_other, in_own, in_other,
    gp_other, scale_other, attended1, wo_other,
    grads, small, small2, small3, normed_own, normed_other, enc_part,
    gp,
):
    frames, width = up.shape[1:]
    share = wo.shape[0]
    scale_own = attention_back(0, scale, up, wo, qkv, invs, probs, gp, first_lanes(frames, share))
    gain_part = None
    for p in (1, 0):
        grad = dot(gp[p], w_own[...], 1, 1) + dot(gp_other[p], w_other[...], 1, 1)
        x = frames_of((in_own, in_other)[p]).astype(f32)
        inverse = lax.rsqrt(jnp.mean(x * x, axis=-1, keepdims=True) + EPS)
        one = jnp.sum(grad * (x * inverse), axis=0, keepdims=True)
        gain_part = one if gain_part is None else gain_part + one
        if p == 0:
            normed_own[...] = grad
        else:
            normed_other[:frames] = grad.astype(bf16)
    weight_grads(grads, normed_t, gp, up, attended_t)
    for p in range(2):
        branch = dot(attended[p], wo[...], 1, 0) + dot(attended1[p], wo_other[...], 1, 0)
        if p == 0:
            enc_part[...] = frames_of(in_own).astype(f32) + branch
        else:
            normed_other[frames + 16 :] = branch.astype(bf16)
    xh, core = place[0], place[1]
    none = jnp.zeros((1, share), f32)
    for r in range(4):
        second = (xh if r < 2 else 1 - xh) == 1
        odd = (core if r % 2 == 0 else 1 - core) == 1

        def block(value):
            low = jnp.where(odd, value[:, share : 2 * share], value[:, :share])
            high = jnp.where(odd, value[:, 3 * share :], value[:, 2 * share : 3 * share])
            return jnp.where(second, high, low)

        tail = (scale_own, none, scale_other[...], none)[r]
        rows = jnp.concatenate([block(act_part[...]), block(gain_part), tail, jnp.zeros((6, share), f32)])
        if r == 1:
            normed_other[frames : frames + 16, :share] = rows.astype(bf16)
        else:
            (small, None, small2, small3)[r][...] = rows
    normed_other[frames : frames + 16, share:] = jnp.zeros((16, width - share), bf16)


def finish_kernel(in_own, gain, grad_own, grad_got, up, enc_part, out):
    x = frames_of(in_own).astype(f32)
    frames, width = x.shape
    inverse = lax.rsqrt(jnp.mean(x * x, axis=-1, keepdims=True) + EPS)
    scaled = gain[...] * (grad_own[...] + grad_got[:frames].astype(f32))
    row_dot = jnp.mean(scaled * x, axis=-1, keepdims=True)
    grad = inverse * scaled - x * (inverse * inverse * inverse * row_dot)
    out[:, :width] = (enc_part[...] + grad_got[frames + 16 :].astype(f32)).astype(bf16)
    out[:, width : 2 * width] = (up[0].astype(f32) + grad).astype(bf16)


VMEM = pl.BlockSpec(memory_space=pltpu.VMEM)
SMEM = pl.BlockSpec(memory_space=pltpu.SMEM)


def call(kernel, scalars, arrays, outs, flops, scratch=()):
    return pl.pallas_call(
        kernel,
        out_shape=[jax.ShapeDtypeStruct(s, d) for s, d in outs],
        in_specs=[SMEM] * len(scalars) + [VMEM] * len(arrays),
        out_specs=[VMEM] * len(outs),
        scratch_shapes=scratch,
        compiler_params=pltpu.CompilerParams(vmem_limit_bytes=60 * 1024 * 1024),
        cost_estimate=pl.CostEstimate(flops=flops, bytes_accessed=flops // 1000, transcendentals=0),
    )(*scalars, *arrays)


def local(
    frames_in,
    norm_gain,
    w_qkv,
    qk_scale,
    w_out,
    w_act,
    action_codes,
    episode_ids,
    cotangent,
    action_cotangent,
):
    fl, patches, width = frames_in.shape
    share = cotangent.shape[2]
    n_tm = lax.axis_size("xl") * lax.axis_size("y") * lax.axis_size("z")
    n_yz = lax.axis_size("y") * lax.axis_size("z")
    frames = fl * n_tm
    group = patches // 4
    tokens = frames * patches
    hd = 64
    xl, xh, core = lax.axis_index("xl"), lax.axis_index("xh"), lax.axis_index("core")
    block = xh * 2 + core
    tm = lax.axis_index(TM)
    gain = norm_gain.reshape(1, width)

    few = jnp.concatenate(
        [w_act.transpose(0, 2, 1).reshape(8, share), jnp.pad(qk_scale[None], ((0, 7), (0, share - 2)))]
    )
    few_got = swap(few, "core")
    few = ordered(few, few_got, core, 0)

    cot = cotangent.reshape(fl, 2, 2, group, share)
    cot = ordered(pick(cot, core, 2), swap(pick(cot, 1 - core, 2), "core"), core, 3)
    sent = pick(frames_in.reshape(fl, 2, 2, group, width), core, 2)
    sent = lax.dynamic_slice_in_dim(sent, xh * 2 * share, 2 * share, 3)
    sent = jnp.concatenate([sent, cot.reshape(fl, 2, group, 2 * share)], axis=-1)
    sent = sent.transpose(1, 2, 0, 3).reshape(2 * n_tm, fl, width)
    in_own = lax.all_to_all(sent, ("xh",) + TM, 0, 0, tiled=True).reshape(2, frames, width)
    in_other = swap(in_own, "core")

    w_own = w_qkv.reshape(width, 3 * share)
    w_other = swap(w_own, "xh")
    wo_other = swap(after(w_out, w_other), "xh")
    place = jnp.stack([xh, core]).astype(jnp.int32)
    few_other = swap(few, "xh")
    act = ordered(few, few_other, xh, 0).reshape(4, 16, share)[:, :8]
    act = act.transpose(1, 0, 2).reshape(8, width)
    act_own = dot(act, w_out.astype(f32), 1, 1, precision=HIGHEST)
    act_other = swap(act_own, "xh")
    scale = jnp.concatenate([qk_scale, pick(few_other, core, 0)[8, :2]])

    ids_row, ids_col = episode_ids[None], episode_ids[:, None]
    (
        normed, qkv0, qkv1, invs0, invs1, probs0, probs1, attended0, attended1, part8
    ) = call(
        forward_kernel,
        (scale,),
        (in_own, in_other, gain, w_own, w_other, ids_row, ids_col, act, act_own, act_other),
        (
            ((2, frames, width), bf16),
            ((2, 3, frames, share), bf16),
            ((2, 3, frames, share), bf16),
            ((2, frames, 4), f32),
            ((2, frames, 4), f32),
            ((2, 2, frames, frames), f32),
            ((2, 2, frames, frames), f32),
            ((2, frames, share), bf16),
            ((2, frames, share), bf16),
            ((8, frames // 2), f32),
        ),
        FORWARD_FLOPS,
    )

    ac_t = jnp.broadcast_to(action_cotangent.T[:, None], (4, n_tm, fl)).reshape(4, frames)
    ac_t = jnp.where(jnp.arange(frames)[None] // fl == tm, ac_t, 0.0)
    ac8 = jnp.concatenate([ac_t[:, : frames // 2], ac_t[:, frames // 2 :]])
    part8 = part8 + swap(part8, "core")
    packed = jnp.concatenate([part8, ac8])
    from_xh = swap(part8, "xh")
    from_xl = swap(packed, "xl")
    from_both = lax.ppermute(part8, ("xl", "xh"), [(0, 3), (1, 2), (2, 1), (3, 0)])
    far = jnp.concatenate([from_xh + from_both, jnp.zeros_like(ac8)])
    sums = (packed + from_xl) + far
    packed = jnp.broadcast_to(sums[None], (n_yz, 16, frames // 2))
    packed = lax.all_to_all(packed, YZ, 0, 0, tiled=True)

    normed_t, attended0_t, attended1_t = call(
        prepare_kernel,
        (),
        (after(normed, sums), attended0, attended1),
        (((2, width, frames), bf16), ((2, share, frames), bf16), ((2, share, frames), bf16)),
        FORWARD_FLOPS,
    )
    bounded, act_part, up, gp_other, grads_other, scale_other = call(
        other_kernel,
        (scale,),
        (
            packed, in_own, in_other, act, w_out, wo_other, qkv1, invs1, probs1, attended0, attended1, normed_t, attended1_t,
        ),
        (
            ((4, frames), f32),
            ((8, width), f32),
            ((2, frames, width), bf16),
            ((2, frames, 3 * share), bf16),
            ((width // 2, 2 * width), bf16),
            ((1, share), f32),
        ),
        BACKWARD_FLOPS,
        scratch=[pltpu.VMEM((frames, width), f32)],
    )
    grads_got = swap(grads_other, "xh")
    grads_own, small, small2, small3, normed_own, normed_other, enc_part = call(
        own_kernel,
        (scale, place),
        (
            act_part, up, w_out, qkv0, invs0, probs0, attended0, normed_t, attended0_t, w_own, w_other, in_own, in_other,
            gp_other, scale_other, attended1, wo_other,
        ),
        (
            ((width // 2, 2 * width), f32),
            ((16, share), f32),
            ((16, share), f32),
            ((16, share), f32),
            ((frames, width), f32),
            ((2 * frames + 16, width), bf16),
            ((frames, width), f32),
        ),
        BACKWARD_FLOPS,
        scratch=[pltpu.VMEM((2, frames, 3 * share), bf16)],
    )

    normed_got = swap(normed_other, "core")
    (both_out,) = call(
        finish_kernel,
        (),
        (in_own, gain, normed_own, normed_got, up, enc_part),
        (((frames, 2 * width), bf16),),
        10 * frames * width,
    )
    far = lax.ppermute(small3, ("xh", "core"), [(0, 3), (1, 2), (2, 1), (3, 0)])
    small = (small + normed_got[frames : frames + 16, :share].astype(f32)) + (swap(small2, "xh") + far)
    small = jnp.pad(small.astype(bf16), ((0, frames - 16), (0, 0)))
    def half_of(index):
        own = lax.dynamic_slice_in_dim(grads_own, index * width, width, 1)
        return own + lax.dynamic_slice_in_dim(grads_got, index * width, width, 1).astype(f32)

    from_xl = swap(half_of(1 - xl).astype(bf16), "xl")
    grads = (half_of(xl) + from_xl.astype(f32)).astype(bf16)
    both_out = jnp.concatenate([both_out, grads, small], axis=1)
    home = lax.all_to_all(both_out.reshape(n_tm, fl, 3 * width + share), TM, 0, 0, tiled=True)
    summed = jnp.sum(home[:, :, 2 * width :].astype(f32).reshape(2, n_yz, fl, width + share), axis=1)
    few = summed[0, :, width:] + summed[1, :, width:]
    summed = jnp.concatenate([summed[0, :, :width], summed[1, :, :width], few], axis=1).astype(bf16)
    copies = jnp.broadcast_to(summed[None], (n_tm, *summed.shape))
    summed = lax.all_to_all(copies, TM, 0, 0, tiled=True).reshape(frames, 2 * width + share)
    home = after(home[:, :, : 2 * width], copies)
    home = home.reshape(group, fl, 2, 2, 2, share)

    def block_of(x_index, core_index):
        return pick(pick(home, x_index, 3), core_index, 3)

    from_core = swap(block_of(xh, 1 - core), "core")
    from_xh = swap(block_of(1 - xh, core), "xh")
    from_both = lax.ppermute(block_of(1 - xh, 1 - core), ("xh", "core"), [(0, 3), (1, 2), (2, 1), (3, 0)])
    near = ordered(block_of(xh, core), from_core, core, 0)
    home = ordered(near, ordered(from_xh, from_both, core, 0), xh, 0)
    home = home.transpose(4, 3, 0, 1, 2, 5).reshape(2, fl, patches, share)
    encoded, grad_frames = home[0], home[1]

    half_level, offsets, widths = (np.array(v, np.float32)[:, None] for v in (HALF, OFFSET, WIDTH))
    bases = jnp.array([1, 8, 40, 200], dtype=jnp.int32)[:, None]
    radices = jnp.array([8, 5, 5, 5], dtype=jnp.int32)[:, None]
    digits = action_codes[None, :] // bases % radices
    bounded_own = lax.dynamic_slice_in_dim(bounded, tm * fl, fl, 1)
    quant_gap = ((digits.astype(f32) - widths) / widths - bounded_own).T

    norm_factor = 1.0 / math.sqrt(tokens)
    qkv_halves = jnp.concatenate([summed[:, : 3 * share], summed[:, 3 * share : 6 * share]])
    grad_qkv = qkv_halves.astype(f32).reshape(width, 3, share) * norm_factor
    out_halves = [summed[k * share : (k + 1) * share, 6 * share : 2 * width] for k in range(2)]
    grad_out = jnp.concatenate(out_halves, axis=1).astype(f32) * norm_factor
    small = summed[:16, 2 * width :].astype(f32)
    grad_act = small[:8].reshape(2, 4, share).transpose(0, 2, 1) * (1.0 / math.sqrt(frames) / patches)
    grad_gain = small[8] * norm_factor
    grad_qk_scale = small[9, :2] * (norm_factor / math.sqrt(hd))
    return (encoded, quant_gap, grad_frames, grad_gain, grad_qkv, grad_qk_scale, grad_out, grad_act)


def solution(mesh):
    fine = Mesh(mesh.devices.reshape(2, 4, 8, 2, 2), ("xl", "y", "z", "xh", "core"))
    head = ("xh", "core")
    in_specs = (
        P(TM, None, None),
        P(),
        P(None, None, head),
        P(head),
        P(head, None),
        P(None, head, None),
        P(TM),
        P(),
        P(TM, None, head),
        P(TM, None),
    )
    out_specs = (
        P(TM, None, head),
        P(TM, None),
        P(TM, None, head),
        P(head),
        P(None, None, head),
        P(head),
        P(head, None),
        P(None, head, None),
    )
    return jax.shard_map(local, mesh=fine, in_specs=in_specs, out_specs=out_specs, check_vma=False)
```

```python
import math

import jax
import jax.numpy as jnp
import numpy as np
from jax import lax
from jax.experimental import pallas as pl
from jax.experimental.pallas import tpu as pltpu
from jax.sharding import Mesh
from jax.sharding import PartitionSpec as P

LAG = 16
EPS = 1e-06
HIGHEST = lax.Precision.HIGHEST
TM = ("xl", "y", "z")
YZ = ("y", "z")
bf16 = jnp.bfloat16
f32 = jnp.float32
FORWARD_FLOPS = 1_000
BACKWARD_FLOPS = 5_000_000_000


def swap(value, axis):
    return lax.ppermute(value, axis, [(0, 1), (1, 0)])


def ordered(own, other, index, axis):
    first = jnp.where(index == 0, own, other)
    second = jnp.where(index == 0, other, own)
    return jnp.stack([first, second], axis=axis)


def pick(value, index, axis):
    return lax.dynamic_index_in_dim(value, index, axis, keepdims=False)


def after(value, *earlier):
    return lax.optimization_barrier((value, *earlier))[0]


HALF = [(n - 1.0) * (1.0 - 0.001) / 2.0 for n in (8.0, 5.0, 5.0, 5.0)]
OFFSET = [0.5, 0.0, 0.0, 0.0]
WIDTH = [4.0, 2.0, 2.0, 2.0]
SHIFT = [0.5 * math.log((a + b) / (a - b)) for a, b in zip(HALF, OFFSET)]


def by_level(values, shape):
    row = lax.broadcasted_iota(jnp.int32, shape, 0)
    return jnp.where(row == 0, values[0], values[1]).astype(f32)


def dot(a, b, ca, cb, **kw):
    return lax.dot_general(a, b, (((ca,), (cb,)), ((), ())), preferred_element_type=f32, **kw)


def pieces(values):
    high = values.astype(bf16).astype(f32)
    middle = (values - high).astype(bf16).astype(f32)
    return high, middle, (values - high - middle).astype(bf16).astype(f32)


def dot_wide(few, many, ca, cb):
    rows = few.shape[0]
    out = dot(jnp.concatenate(pieces(few)).astype(bf16), many, ca, cb)
    return out[:rows] + (out[rows : 2 * rows] + out[2 * rows :])


def per_head(values, first):
    one = jnp.sum(jnp.where(first, values, 0.0), axis=-1, keepdims=True)
    two = jnp.sum(jnp.where(first, 0.0, values), axis=-1, keepdims=True)
    return one, two


def attention_forward(b, scale, normed, w, ids_row, ids_col, qkv, invs, probs, attended):
    frames, share = qkv.shape[2:]
    hd, mid = share // 2, frames // 2
    first = first_lanes(frames, share)
    t = lax.broadcasted_iota(jnp.int32, (frames, frames), 0)
    u = lax.broadcasted_iota(jnp.int32, (frames, frames), 1)
    visible = jnp.logical_and(ids_col[...] == ids_row[...], u <= t)
    for p in range(2):
        raw = dot(normed[p], w[...], 1, 0)
        parts = []
        for k in range(2):
            one = raw[:, k * share : (k + 1) * share]
            sums = per_head(one * one, first)
            inv0 = lax.rsqrt(sums[0] * (1.0 / hd) + EPS)
            inv1 = lax.rsqrt(sums[1] * (1.0 / hd) + EPS)
            invs[p, :, k * 2 : k * 2 + 1] = inv0
            invs[p, :, k * 2 + 1 : k * 2 + 2] = inv1
            parts.append((one * jnp.where(first, inv0, inv1)).astype(bf16))
        parts.append(raw[:, 2 * share :].astype(bf16))
        query, keys, values = parts
        for k in range(3):
            qkv[p, k] = parts[k]
        zero = jnp.zeros_like(keys)
        mixed = [None, None]
        for h in range(2):
            mask = first if h == 0 else jnp.logical_not(first)
            keys_h, values_h = jnp.where(mask, keys, zero), jnp.where(mask, values, zero)
            factor = scale[b * 2 + h] * (1.0 / math.sqrt(hd))
            for k, (rows, seen) in enumerate(((slice(0, mid), mid), (slice(mid, frames), frames))):
                dots = dot(query[rows], keys_h[:seen], 1, 1)
                weights = jnp.where(visible[rows, :seen], jnp.exp(dots * factor), 0.0)
                prob = weights * (1.0 / jnp.sum(weights, axis=-1, keepdims=True))
                probs[p, h, rows, :seen] = prob
                one = dot(prob.astype(bf16), values_h[:seen], 1, 0)
                mixed[k] = one if mixed[k] is None else mixed[k] + one
        attended[p] = jnp.concatenate(mixed).astype(bf16)


def forward_kernel(
    scale, in_own, in_other, gain, w_own, w_other, ids_row, ids_col, act, act_own, act_other,
    normed, qkv0, qkv1, invs0, invs1, probs0, probs1, attended0, attended1, part8,
):
    frames = in_own.shape[1]
    for p in range(2):
        x = frames_of((in_own, in_other)[p]).astype(f32)
        inverse = lax.rsqrt(jnp.mean(x * x, axis=-1, keepdims=True) + EPS)
        normed[p] = (x * inverse * gain[...]).astype(bf16)
    attention_forward(0, scale, normed, w_own, ids_row, ids_col, qkv0, invs0, probs0, attended0)
    attention_forward(1, scale, normed, w_other, ids_row, ids_col, qkv1, invs1, probs1, attended1)
    terms = dot_wide(act[...], frames_of(in_own), 1, 1)
    for act_out, att in ((act_own, attended0), (act_other, attended1)):
        terms = terms + (dot_wide(act_out[...], att[0], 1, 1) + dot_wide(act_out[...], att[1], 1, 1))
    terms = terms * (1.0 / 256.0)
    moved = pltpu.roll(terms, frames - LAG, 1)
    moved = jnp.where(lax.broadcasted_iota(jnp.int32, moved.shape, 1) < frames - LAG, moved, 0.0)
    part = terms[:4] + moved[4:]
    part8[0:4] = part[:, : frames // 2]
    part8[4:8] = part[:, frames // 2 :]


def attention_back(b, scale, up, wo, qkv, invs, probs, gp, first):
    share, frames = wo.shape[0], up.shape[1]
    hd, mid = share // 2, frames // 2
    sums = [None, None]
    factor = jnp.where(
        first[:1], scale[b * 2] * (1.0 / math.sqrt(hd)), scale[b * 2 + 1] * (1.0 / math.sqrt(hd))
    )
    for p in range(2):
        query, keys, values = qkv[p, 0], qkv[p, 1], qkv[p, 2]
        zero = jnp.zeros_like(keys)
        grad_att = dot(up[p], wo[...], 1, 1).astype(bf16)
        grad_q, low, high = [None, None], [None, None], [None, None]

        def add(old, new):
            return new if old is None else old + new

        for h in range(2):
            mask = first if h == 0 else jnp.logical_not(first)
            query_h, keys_h = jnp.where(mask, query, zero), jnp.where(mask, keys, zero)
            values_h, grad_h = jnp.where(mask, values, zero), jnp.where(mask, grad_att, zero)
            for k, (rows, seen) in enumerate(((slice(0, mid), mid), (slice(mid, frames), frames))):
                grad_probs = dot(grad_att[rows], values_h[:seen], 1, 1)
                prob = probs[p, h, rows, :seen]
                inner = jnp.sum(grad_probs * prob, axis=-1, keepdims=True)
                grad_scores = (prob * (grad_probs - inner)).astype(bf16)
                grad_q[k] = add(grad_q[k], dot(grad_scores, keys_h[:seen], 1, 0))
                target = (low, high)[k]
                target[0] = add(target[0], dot(grad_scores, query_h[rows], 0, 0))
                target[1] = add(target[1], dot(prob.astype(bf16), grad_h[rows], 0, 0))
        grad_q = jnp.concatenate(grad_q)
        grad_k, grad_v = (jnp.concatenate([low[j] + high[j][:mid], high[j][mid:]]) for j in range(2))
        for k in range(2):
            grad, base = ((grad_q, query), (grad_k, keys))[k]
            base = base.astype(f32)
            one, two = per_head(grad * base, first)
            if k == 0:
                one_sum, two_sum = jnp.sum(one, axis=0, keepdims=True), jnp.sum(two, axis=0, keepdims=True)
                sums[0] = one_sum if sums[0] is None else sums[0] + one_sum
                sums[1] = two_sum if sums[1] is None else sums[1] + two_sum
            mean = jnp.where(first, one, two) * (1.0 / hd)
            inv = jnp.where(first, invs[p, :, 2 * k : 2 * k + 1], invs[p, :, 2 * k + 1 : 2 * k + 2])
            gp[p, :, k * share : (k + 1) * share] = (factor * inv * (grad - base * mean)).astype(bf16)
        gp[p, :, 2 * share : 3 * share] = grad_v.astype(bf16)
    lane = lax.broadcasted_iota(jnp.int32, (1, share), 1)
    return jnp.where(lane == 0, sums[0], 0.0) + jnp.where(lane == 1, sums[1], 0.0)


def prepare_kernel(normed, attended0, attended1, normed_t, attended0_t, attended1_t):
    for p in range(2):
        normed_t[p] = normed[p].T
        attended0_t[p] = attended0[p].T
        attended1_t[p] = attended1[p].T


def weight_grads(target, normed_t, gp, up, attended_t):
    split = gp.shape[2]
    half, share = normed_t.shape[1] // 2, attended_t.shape[1]
    qkv_part = dot(normed_t[0], gp[0], 1, 0) + dot(normed_t[1], gp[1], 1, 0)
    out_part = dot(attended_t[0], up[0], 1, 0) + dot(attended_t[1], up[1], 1, 0)
    for k in range(2):
        target[:, k * split : (k + 1) * split] = qkv_part[k * half : (k + 1) * half].astype(target.dtype)
        target[k * share : (k + 1) * share, 2 * split :] = out_part[:, k * half : (k + 1) * half].astype(target.dtype)


def frames_of(home):
    half = home.shape[2] // 2
    return jnp.concatenate([home[0, :, :half], home[1, :, :half]], axis=1)


def first_lanes(frames, share):
    return lax.broadcasted_iota(jnp.int32, (frames, share), 1) < share // 2


def other_kernel(
    scale, packed, in_own, in_other, act, wo_own, wo, qkv, invs, probs, attended0, attended, normed_t, attended_t,
    bounded_out, act_part, up, gp, grads, scale_row,
    pooled,
):
    frames, width = up.shape[1:]
    share = wo.shape[0]
    summed = jnp.sum(packed[...], axis=0)
    latent = jnp.concatenate([summed[0:4], summed[4:8]], axis=1)
    cot_act = jnp.concatenate([summed[8:12], summed[12:16]], axis=1)
    shape = latent.shape
    half, offset, widths = by_level(HALF, shape), by_level(OFFSET, shape), by_level(WIDTH, shape)
    curve = jnp.tanh(latent + by_level(SHIFT, shape))
    bounded_out[...] = (curve * half - offset) / widths
    grad_latent = cot_act * (half / widths) * (1.0 - curve * curve)
    moved = pltpu.roll(grad_latent, LAG, 1)
    moved = jnp.where(lax.broadcasted_iota(jnp.int32, shape, 1) >= LAG, moved, 0.0)
    eight = jnp.concatenate([grad_latent, moved], axis=0)
    left, right = pieces(eight), pieces(act[...])
    pairs = ((0, 0), (0, 1), (1, 0), (1, 1), (0, 2), (2, 0))
    lefts = jnp.concatenate([left[i] for i, _ in pairs]).T.astype(bf16)
    rights = jnp.concatenate([right[j] for _, j in pairs]).astype(bf16)
    pooled[...] = dot(lefts, rights, 1, 0) * (1.0 / 256.0)
    half = width // 2
    for p in range(2):
        for r in range(2):
            cols = slice(r * half, (r + 1) * half)
            cot = (in_own, in_other)[p][r, :, half:].astype(f32)
            up[p, :, cols] = (cot + pooled[:, cols]).astype(bf16)
    scale_row[...] = attention_back(1, scale, up, wo, qkv, invs, probs, gp, first_lanes(frames, share))
    weight_grads(grads, normed_t, gp, up, attended_t)
    part = dot_wide(eight, frames_of(in_own), 1, 0)
    for att, w in ((attended0, wo_own), (attended, wo)):
        mixed = dot_wide(eight, att[0], 1, 0) + dot_wide(eight, att[1], 1, 0)
        part = part + dot_wide(mixed, w[...], 1, 0)
    act_part[...] = part


def own_kernel(
    scale, place, act_part, up, wo, qkv, invs, probs, attended, normed_t, attended_t, w_own, w_other, in_own, in_other,
    gp_other, scale_other, attended1, wo_other,
    grads, small, small2, small3, normed_own, normed_other, enc_part,
    gp,
):
    frames, width = up.shape[1:]
    share = wo.shape[0]
    scale_own = attention_back(0, scale, up, wo, qkv, invs, probs, gp, first_lanes(frames, share))
    gain_part = None
    for p in (1, 0):
        grad = dot(gp[p], w_own[...], 1, 1) + dot(gp_other[p], w_other[...], 1, 1)
        x = frames_of((in_own, in_other)[p]).astype(f32)
        inverse = lax.rsqrt(jnp.mean(x * x, axis=-1, keepdims=True) + EPS)
        one = jnp.sum(grad * (x * inverse), axis=0, keepdims=True)
        gain_part = one if gain_part is None else gain_part + one
        if p == 0:
            normed_own[...] = grad
        else:
            normed_other[:frames] = grad.astype(bf16)
    weight_grads(grads, normed_t, gp, up, attended_t)
    for p in range(2):
        branch = dot(attended[p], wo[...], 1, 0) + dot(attended1[p], wo_other[...], 1, 0)
        if p == 0:
            enc_part[...] = frames_of(in_own).astype(f32) + branch
        else:
            normed_other[frames + 16 :] = branch.astype(bf16)
    xh, core = place[0], place[1]
    none = jnp.zeros((1, share), f32)
    for r in range(4):
        second = (xh if r < 2 else 1 - xh) == 1
        odd = (core if r % 2 == 0 else 1 - core) == 1

        def block(value):
            low = jnp.where(odd, value[:, share : 2 * share], value[:, :share])
            high = jnp.where(odd, value[:, 3 * share :], value[:, 2 * share : 3 * share])
            return jnp.where(second, high, low)

        tail = (scale_own, none, scale_other[...], none)[r]
        rows = jnp.concatenate([block(act_part[...]), block(gain_part), tail, jnp.zeros((6, share), f32)])
        if r == 1:
            normed_other[frames : frames + 16, :share] = rows.astype(bf16)
        else:
            (small, None, small2, small3)[r][...] = rows
    normed_other[frames : frames + 16, share:] = jnp.zeros((16, width - share), bf16)


def finish_kernel(in_own, gain, grad_own, grad_got, up, enc_part, out):
    x = frames_of(in_own).astype(f32)
    frames, width = x.shape
    inverse = lax.rsqrt(jnp.mean(x * x, axis=-1, keepdims=True) + EPS)
    scaled = gain[...] * (grad_own[...] + grad_got[:frames].astype(f32))
    row_dot = jnp.mean(scaled * x, axis=-1, keepdims=True)
    grad = inverse * scaled - x * (inverse * inverse * inverse * row_dot)
    out[:, :width] = (enc_part[...] + grad_got[frames + 16 :].astype(f32)).astype(bf16)
    out[:, width : 2 * width] = (up[0].astype(f32) + grad).astype(bf16)


VMEM = pl.BlockSpec(memory_space=pltpu.VMEM)
SMEM = pl.BlockSpec(memory_space=pltpu.SMEM)


def call(kernel, scalars, arrays, outs, flops, scratch=()):
    return pl.pallas_call(
        kernel,
        out_shape=[jax.ShapeDtypeStruct(s, d) for s, d in outs],
        in_specs=[SMEM] * len(scalars) + [VMEM] * len(arrays),
        out_specs=[VMEM] * len(outs),
        scratch_shapes=scratch,
        compiler_params=pltpu.CompilerParams(vmem_limit_bytes=60 * 1024 * 1024),
        cost_estimate=pl.CostEstimate(flops=flops, bytes_accessed=flops // 1000, transcendentals=0),
    )(*scalars, *arrays)


def local(
    frames_in,
    norm_gain,
    w_qkv,
    qk_scale,
    w_out,
    w_act,
    action_codes,
    episode_ids,
    cotangent,
    action_cotangent,
):
    fl, patches, width = frames_in.shape
    share = cotangent.shape[2]
    n_tm = lax.axis_size("xl") * lax.axis_size("y") * lax.axis_size("z")
    n_yz = lax.axis_size("y") * lax.axis_size("z")
    frames = fl * n_tm
    group = patches // 4
    tokens = frames * patches
    hd = 64
    xl, xh, core = lax.axis_index("xl"), lax.axis_index("xh"), lax.axis_index("core")
    block = xh * 2 + core
    tm = lax.axis_index(TM)
    gain = norm_gain.reshape(1, width)

    few = jnp.concatenate(
        [w_act.transpose(0, 2, 1).reshape(8, share), jnp.pad(qk_scale[None], ((0, 7), (0, share - 2)))]
    )
    few_got = swap(few, "core")
    few = ordered(few, few_got, core, 0)

    cot = cotangent.reshape(fl, 2, 2, group, share)
    cot = ordered(pick(cot, core, 2), swap(pick(cot, 1 - core, 2), "core"), core, 3)
    sent = pick(frames_in.reshape(fl, 2, 2, group, width), core, 2)
    sent = lax.dynamic_slice_in_dim(sent, xh * 2 * share, 2 * share, 3)
    sent = jnp.concatenate([sent, cot.reshape(fl, 2, group, 2 * share)], axis=-1)
    sent = sent.transpose(1, 2, 0, 3).reshape(2 * n_tm, fl, width)
    in_own = lax.all_to_all(sent, ("xh",) + TM, 0, 0, tiled=True).reshape(2, frames, width)
    in_other = swap(in_own, "core")

    w_own = w_qkv.reshape(width, 3 * share)
    w_other = swap(w_own, "xh")
    wo_other = swap(after(w_out, w_other), "xh")
    place = jnp.stack([xh, core]).astype(jnp.int32)
    few_other = swap(few, "xh")
    act = ordered(few, few_other, xh, 0).reshape(4, 16, share)[:, :8]
    act = act.transpose(1, 0, 2).reshape(8, width)
    act_own = dot(act, w_out.astype(f32), 1, 1, precision=HIGHEST)
    act_other = swap(act_own, "xh")
    scale = jnp.concatenate([qk_scale, pick(few_other, core, 0)[8, :2]])

    ids_row, ids_col = episode_ids[None], episode_ids[:, None]
    (
        normed, qkv0, qkv1, invs0, invs1, probs0, probs1, attended0, attended1, part8
    ) = call(
        forward_kernel,
        (scale,),
        (in_own, in_other, gain, w_own, w_other, ids_row, ids_col, act, act_own, act_other),
        (
            ((2, frames, width), bf16),
            ((2, 3, frames, share), bf16),
            ((2, 3, frames, share), bf16),
            ((2, frames, 4), f32),
            ((2, frames, 4), f32),
            ((2, 2, frames, frames), f32),
            ((2, 2, frames, frames), f32),
            ((2, frames, share), bf16),
            ((2, frames, share), bf16),
            ((8, frames // 2), f32),
        ),
        FORWARD_FLOPS,
    )

    ac_t = jnp.broadcast_to(action_cotangent.T[:, None], (4, n_tm, fl)).reshape(4, frames)
    ac_t = jnp.where(jnp.arange(frames)[None] // fl == tm, ac_t, 0.0)
    ac8 = jnp.concatenate([ac_t[:, : frames // 2], ac_t[:, frames // 2 :]])
    part8 = part8 + swap(part8, "core")
    packed = jnp.concatenate([part8, ac8])
    from_xh = swap(part8, "xh")
    from_xl = swap(packed, "xl")
    from_both = lax.ppermute(part8, ("xl", "xh"), [(0, 3), (1, 2), (2, 1), (3, 0)])
    far = jnp.concatenate([from_xh + from_both, jnp.zeros_like(ac8)])
    sums = (packed + from_xl) + far
    packed = jnp.broadcast_to(sums[None], (n_yz, 16, frames // 2))
    packed = lax.all_to_all(packed, YZ, 0, 0, tiled=True)

    normed_t, attended0_t, attended1_t = call(
        prepare_kernel,
        (),
        (after(normed, sums), attended0, attended1),
        (((2, width, frames), bf16), ((2, share, frames), bf16), ((2, share, frames), bf16)),
        FORWARD_FLOPS,
    )
    bounded, act_part, up, gp_other, grads_other, scale_other = call(
        other_kernel,
        (scale,),
        (
            packed, in_own, in_other, act, w_out, wo_other, qkv1, invs1, probs1, attended0, attended1, normed_t, attended1_t,
        ),
        (
            ((4, frames), f32),
            ((8, width), f32),
            ((2, frames, width), bf16),
            ((2, frames, 3 * share), bf16),
            ((width // 2, 2 * width), bf16),
            ((1, share), f32),
        ),
        BACKWARD_FLOPS,
        scratch=[pltpu.VMEM((frames, width), f32)],
    )
    grads_got = swap(grads_other, "xh")
    grads_own, small, small2, small3, normed_own, normed_other, enc_part = call(
        own_kernel,
        (scale, place),
        (
            act_part, up, w_out, qkv0, invs0, probs0, attended0, normed_t, attended0_t, w_own, w_other, in_own, in_other,
            gp_other, scale_other, attended1, wo_other,
        ),
        (
            ((width // 2, 2 * width), bf16),
            ((16, share), f32),
            ((16, share), f32),
            ((16, share), f32),
            ((frames, width), f32),
            ((2 * frames + 16, width), bf16),
            ((frames, width), f32),
        ),
        BACKWARD_FLOPS,
        scratch=[pltpu.VMEM((2, frames, 3 * share), bf16)],
    )

    normed_got = swap(normed_other, "core")
    (both_out,) = call(
        finish_kernel,
        (),
        (in_own, gain, normed_own, normed_got, up, enc_part),
        (((frames, 2 * width), bf16),),
        10 * frames * width,
    )
    far = lax.ppermute(small3, ("xh", "core"), [(0, 3), (1, 2), (2, 1), (3, 0)])
    small = (small + normed_got[frames : frames + 16, :share].astype(f32)) + (swap(small2, "xh") + far)
    small = jnp.pad(small.astype(bf16), ((0, frames - 16), (0, 0)))
    def half_of(index):
        own = lax.dynamic_slice_in_dim(grads_own, index * width, width, 1)
        return own.astype(f32) + lax.dynamic_slice_in_dim(grads_got, index * width, width, 1).astype(f32)

    from_xl = swap(half_of(1 - xl).astype(bf16), "xl")
    grads = (half_of(xl) + from_xl.astype(f32)).astype(bf16)
    both_out = jnp.concatenate([both_out, grads, small], axis=1)
    home = lax.all_to_all(both_out.reshape(n_tm, fl, 3 * width + share), TM, 0, 0, tiled=True)
    summed = jnp.sum(home[:, :, 2 * width :].astype(f32).reshape(2, n_yz, fl, width + share), axis=1)
    few = summed[0, :, width:] + summed[1, :, width:]
    summed = jnp.concatenate([summed[0, :, :width], summed[1, :, :width], few], axis=1).astype(bf16)
    copies = jnp.broadcast_to(summed[None], (n_tm, *summed.shape))
    summed = lax.all_to_all(copies, TM, 0, 0, tiled=True).reshape(frames, 2 * width + share)
    home = after(home[:, :, : 2 * width], copies)
    home = home.reshape(group, fl, 2, 2, 2, share)

    def block_of(x_index, core_index):
        return pick(pick(home, x_index, 3), core_index, 3)

    from_core = swap(block_of(xh, 1 - core), "core")
    from_xh = swap(block_of(1 - xh, core), "xh")
    from_both = lax.ppermute(block_of(1 - xh, 1 - core), ("xh", "core"), [(0, 3), (1, 2), (2, 1), (3, 0)])
    near = ordered(block_of(xh, core), from_core, core, 0)
    home = ordered(near, ordered(from_xh, from_both, core, 0), xh, 0)
    home = home.transpose(4, 3, 0, 1, 2, 5).reshape(2, fl, patches, share)
    encoded, grad_frames = home[0], home[1]

    half_level, offsets, widths = (np.array(v, np.float32)[:, None] for v in (HALF, OFFSET, WIDTH))
    bases = jnp.array([1, 8, 40, 200], dtype=jnp.int32)[:, None]
    radices = jnp.array([8, 5, 5, 5], dtype=jnp.int32)[:, None]
    digits = action_codes[None, :] // bases % radices
    bounded_own = lax.dynamic_slice_in_dim(bounded, tm * fl, fl, 1)
    quant_gap = ((digits.astype(f32) - widths) / widths - bounded_own).T

    norm_factor = 1.0 / math.sqrt(tokens)
    qkv_halves = jnp.concatenate([summed[:, : 3 * share], summed[:, 3 * share : 6 * share]])
    grad_qkv = qkv_halves.astype(f32).reshape(width, 3, share) * norm_factor
    out_halves = [summed[k * share : (k + 1) * share, 6 * share : 2 * width] for k in range(2)]
    grad_out = jnp.concatenate(out_halves, axis=1).astype(f32) * norm_factor
    small = summed[:16, 2 * width :].astype(f32)
    grad_act = small[:8].reshape(2, 4, share).transpose(0, 2, 1) * (1.0 / math.sqrt(frames) / patches)
    grad_gain = small[8] * norm_factor
    grad_qk_scale = small[9, :2] * (norm_factor / math.sqrt(hd))
    return (encoded, quant_gap, grad_frames, grad_gain, grad_qkv, grad_qk_scale, grad_out, grad_act)


def solution(mesh):
    fine = Mesh(mesh.devices.reshape(2, 4, 8, 2, 2), ("xl", "y", "z", "xh", "core"))
    head = ("xh", "core")
    in_specs = (
        P(TM, None, None),
        P(),
        P(None, None, head),
        P(head),
        P(head, None),
        P(None, head, None),
        P(TM),
        P(),
        P(TM, None, head),
        P(TM, None),
    )
    out_specs = (
        P(TM, None, head),
        P(TM, None),
        P(TM, None, head),
        P(head),
        P(None, None, head),
        P(head),
        P(head, None),
        P(None, head, None),
    )
    return jax.shard_map(local, mesh=fine, in_specs=in_specs, out_specs=out_specs, check_vma=False)
```
